128 devices in a mesh: row: 8 (over y, z_hi), col: 16 (over x, z_lo, core).
Axes of the slice: x: 4, y: 4, z: 4 (z_hi: 2, z_lo: 2; z = z_hi * 2 + z_lo), core: 2. Of those that a mesh axis runs over, the one named last changes fastest.
Arguments:
- source_table: bfloat16 [8, 2048, 400], P('row', 'col'), may hold values from -3 to 3
- dest_table: bfloat16 [16, 2048, 400], P('col', 'row'), may hold values from -3 to 3
- relations: float32 [1345, 400], replicated, may hold values from -4 to 4
- rel_history: float32 [1345, 400], replicated, may hold values from 0.5 to 5
- src_ids: int32 [8, 16, 2, 4000], P('row', 'col'), may hold values from 0 to 2047
- rel_ids: int32 [8, 16, 2, 4000], P('row', 'col'), may hold values from 0 to 1344
- dst_ids: int32 [8, 16, 2, 4000], P('row', 'col'), may hold values from 0 to 2047
- neg_ids: int32 [8, 16, 2, 4, 1000], P('row', 'col'), may hold values from 0 to 2047
- counts: int32 [8, 16, 2], P('row', 'col'), may hold values from 500 to 4000, as said below
Outputs:
- source_out: bfloat16 [8, 2048, 400], P('row', 'col')
- dest_out: bfloat16 [16, 2048, 400], P('col', 'row')
- relations_out: float32 [1345, 400], replicated
- history_out: float32 [1345, 400], replicated
The draws below stay inside these ranges and needn't reach their ends.
Inputs may be any that keep to these rules, and one draw needn't show every extreme that they name: `counts`: live edges come first in each list; some bucket holds 4000 live edges in every draw.
All inputs are finite; a program needn't handle non-finite values.
Results may differ from the reference program's by a relative error of at most 0.029.
Values may be sent and summed in bfloat16 or wider, within the bound.
A program may use at most 128 MiB of HBM per device.

```python
import math
import jax
import jax.numpy as jnp
import numpy as np
from jax import lax

W = 400
R = 1345
PART = 2048
NEG = 1000
GROUPS = 4
EDGES = 4000
HALF_COL = 8
N_ROW = 8
N_COL = 16


def draw_counts(key, part):
    key = jax.random.fold_in(key, 7)
    first_key, second_key = jax.random.split(key)
    total = N_ROW * N_COL * 2
    place = jnp.arange(total, dtype=jnp.int32)
    device = place // 2
    trend = 8 * device // max(N_ROW * N_COL - 1, 1)
    level = jax.random.randint(first_key, (total,), 0, 8) + trend
    level = jnp.minimum(level, 15)
    chosen = jax.random.randint(second_key, (), 0, total)
    level = jnp.where(place == chosen, 15, level)
    lowest = EDGES // 8
    values = lowest + (EDGES - lowest) * level * level * level // 3375
    return values.reshape(N_ROW, N_COL, 2).astype(jnp.int32)


def set_ends(values, key, smallest, high):
    dims = values.shape
    index_at = [jax.random.randint(jax.random.fold_in(key, axis), (), 0, dims[axis]) for axis in range(len(dims))]
    values = values.at[tuple(index_at)].set(smallest)
    longest = dims.index(max(dims))
    index_at[longest] = (index_at[longest] + 1) % dims[longest]
    return values.at[tuple(index_at)].set(high)


def steps_of(key, extent, shards, least, top_value):
    def one(axis_at, parts):
        draws = jax.random.uniform(jax.random.fold_in(jax.random.fold_in(key, 6), axis_at), (parts,), jnp.float32, least / len(shards), top_value / len(shards))
        return jnp.repeat(jnp.exp(draws), extent[axis_at] // parts).reshape((-1,) + (1,) * (len(extent) - axis_at - 1))

    gain = one(*shards[0])
    for cut in shards[1:]:
        gain = gain * one(*cut)
    return gain


def rank_bounds(amount, lean):
    weights = [(1 << 20) // math.isqrt(rank ** lean) + 1 for rank in range(1, amount + 1)]
    scale = 1 + sum(weights) // (1 << 30)
    return np.cumsum(np.array([max(1, weight // scale) for weight in weights]))


def ranked_ids(rng, extent, count, lean):
    listing = rank_bounds(count, lean)
    pick = jax.random.randint(jax.random.fold_in(rng, 1), extent, 0, int(listing[count - 1]))
    standing = jnp.searchsorted(jnp.asarray(listing, jnp.int32), pick, side="right")
    return jax.random.permutation(jax.random.fold_in(rng, 2), count)[standing].astype(jnp.int32)


def scatter_about(key, dims, scale, limit, cuts=(), kind=jnp.bfloat16):
    gain = steps_of(key, dims, cuts, -0.22, 0.18) if cuts else 1.0
    values = jax.random.normal(key, dims, jnp.float32) * scale * gain
    return jnp.minimum(jnp.maximum(values, -limit), limit).astype(kind)


def setup_inputs(seed: int = 0) -> dict:
    arg_keys = jax.random.split(jax.random.key(seed), 10)
    return {
        "source_table": scatter_about(arg_keys[0], (N_ROW, PART, W), 0.5, 3.0, ((0, 8), (1, 16))),
        "dest_table": scatter_about(arg_keys[1], (N_COL, PART, W), 0.5, 3.0, ((0, 16), (1, 8))),
        "relations": scatter_about(arg_keys[2], (R, W), 1.0, 4.0, (), jnp.float32),
        "rel_history": jnp.clip(jnp.exp(jax.random.uniform(arg_keys[3], (R, W), jnp.float32, math.log(0.5), math.log(5.0))), 0.5, 5.0),
        "src_ids": set_ends(jax.random.randint(arg_keys[4], (N_ROW, N_COL, 2, EDGES), 0, PART), jax.random.fold_in(arg_keys[4], 1), 0, PART - 1).astype(jnp.int32),
        "rel_ids": set_ends(ranked_ids(arg_keys[5], (N_ROW, N_COL, 2, EDGES), R, 2), jax.random.fold_in(arg_keys[5], 3), 0, R - 1).astype(jnp.int32),
        "dst_ids": set_ends(jax.random.randint(arg_keys[6], (N_ROW, N_COL, 2, EDGES), 0, PART), jax.random.fold_in(arg_keys[6], 1), 0, PART - 1).astype(jnp.int32),
        "neg_ids": set_ends(jax.random.randint(arg_keys[7], (N_ROW, N_COL, 2, GROUPS, NEG), 0, PART), jax.random.fold_in(arg_keys[7], 1), 0, PART - 1).astype(jnp.int32),
        "counts": draw_counts(jax.random.fold_in(arg_keys[9], 71), 0),
    }


entity_rate = 0.3
relation_rate = 0.5

def block_terms(position, totals, src_block, dst_block, relations, src_rows, rel_rows, dst_rows, neg_table, live_edges):
    grad_src, grad_dst, grad_rel = totals
    position = jnp.asarray(position).astype(jnp.int32)
    edges_per = src_rows.shape[0] // neg_table.shape[0]
    negs_per = neg_table.shape[1]
    offset = position * edges_per
    src_pick = lax.dynamic_slice_in_dim(src_rows, offset, edges_per)
    rel_pick = lax.dynamic_slice_in_dim(rel_rows, offset, edges_per)
    dst_pick = lax.dynamic_slice_in_dim(dst_rows, offset, edges_per)
    neg_pick = lax.dynamic_index_in_dim(neg_table, position, 0, keepdims=False)
    alive = (offset + jnp.arange(edges_per, dtype=jnp.int32) < live_edges).astype(jnp.float32)
    source = src_block[src_pick].astype(jnp.float32)
    relation = relations[rel_pick]
    target = dst_block[dst_pick].astype(jnp.float32)
    negatives = dst_block[neg_pick]
    half_width = source.shape[1] // 2
    src_re, src_im = (source[:, :half_width], source[:, half_width:])
    rel_re, rel_im = (relation[:, :half_width], relation[:, half_width:])
    rotated = jnp.concatenate([src_re * rel_re - src_im * rel_im, src_re * rel_im + src_im * rel_re], axis=1)
    rotated_b = rotated.astype(jnp.bfloat16)
    pos_score = lax.optimization_barrier(jnp.sum(rotated * target, axis=1))
    neg_score = lax.dot_general(rotated_b, negatives, (((1,), (1,)), ((), ())), preferred_element_type=jnp.float32)
    grad_pos = -alive * jax.nn.sigmoid(-pos_score)
    grad_neg = (jax.nn.sigmoid(neg_score) * (alive[:, None] / negs_per)).astype(jnp.bfloat16)
    grad_rot = grad_pos[:, None] * target + jnp.dot(grad_neg, negatives, preferred_element_type=jnp.float32)
    grad_re, grad_im = (grad_rot[:, :half_width], grad_rot[:, half_width:])
    grad_source = jnp.concatenate([grad_re * rel_re + grad_im * rel_im, grad_im * rel_re - grad_re * rel_im], axis=1)
    grad_relation = jnp.concatenate([grad_re * src_re + grad_im * src_im, grad_im * src_re - grad_re * src_im], axis=1)
    grad_negrows = lax.dot_general(grad_neg, rotated_b, (((0,), (0,)), ((), ())), preferred_element_type=jnp.float32)
    grad_src = grad_src.at[src_pick].add(grad_source)
    grad_dst = grad_dst.at[dst_pick].add(grad_pos[:, None] * rotated)
    grad_dst = grad_dst.at[neg_pick].add(grad_negrows)
    grad_rel = grad_rel.at[rel_pick].add(grad_relation)
    return (grad_src, grad_dst, grad_rel)

def rounded(values):
    return lax.optimization_barrier(values.astype(jnp.bfloat16)).astype(jnp.float32)

def reference(source_table, dest_table, relations, rel_history, src_ids, rel_ids, dst_ids, neg_ids, counts):
    source_now = source_table
    dest_now = dest_table
    relation_now = relations
    history = rel_history
    for round_index in range(2):

        def visit(totals, bucket):
            src_sum, dst_sum, rel_sum = totals
            src_part = bucket // N_COL
            dst_col = bucket % N_COL
            if round_index == 0:
                dst_part = dst_col
            else:
                dst_part = jnp.bitwise_xor(dst_col, HALF_COL)
            src_block = source_now[src_part]
            dst_block = dest_now[dst_part]
            src_rows = src_ids[src_part, dst_col, round_index]
            rel_rows = rel_ids[src_part, dst_col, round_index]
            dst_rows = dst_ids[src_part, dst_col, round_index]
            neg_table = neg_ids[src_part, dst_col, round_index]
            live_edges = counts[src_part, dst_col, round_index]
            empty = (jnp.zeros(src_block.shape, jnp.float32), jnp.zeros(dst_block.shape, jnp.float32), jnp.zeros(relation_now.shape, jnp.float32))

            def advance(position, inner):
                return block_terms(position, inner, src_block, dst_block, relation_now, src_rows, rel_rows, dst_rows, neg_table, live_edges)
            grads = lax.fori_loop(0, GROUPS, advance, empty)
            src_sum = src_sum.at[src_part].add(rounded(grads[0]))
            dst_sum = dst_sum.at[dst_part].add(rounded(grads[1]))
            return ((src_sum, dst_sum, rel_sum + grads[2]), None)
        start_sums = (jnp.zeros(source_now.shape, jnp.float32), jnp.zeros(dest_now.shape, jnp.float32), jnp.zeros(relation_now.shape, jnp.float32))
        sums, unused = lax.scan(visit, start_sums, jnp.arange(N_ROW * N_COL, dtype=jnp.int32))
        src_sum, dst_sum, rel_sum = sums
        history = history + rel_sum * rel_sum
        relation_now = relation_now - relation_rate * rel_sum / jnp.sqrt(history)
        source_now = (source_now.astype(jnp.float32) - entity_rate * src_sum).astype(jnp.bfloat16)
        dest_now = (dest_now.astype(jnp.float32) - entity_rate * dst_sum).astype(jnp.bfloat16)
    return (source_now, dest_now, relation_now, history)
```

```python
import functools
import jax
import jax.numpy as jnp
from jax import lax
from jax.experimental import pallas as pl
from jax.experimental.pallas import tpu as pltpu
from jax.sharding import PartitionSpec as P

F32, BF16 = jnp.float32, jnp.bfloat16
MESH = pl.DeviceIdType.MESH
NT = (((1,), (1,)), ((), ()))
entity_rate = 0.3
relation_rate = 0.5
N_ROW, N_COL = 8, 16
HALF_COL = 8
TILE, LIVE = 512, 500
TILES = 8
CHUNK = 256
REL_CUT = 96
REL_ROWS = REL_CUT * N_COL
VMEM_BYTES = 60 * 2**20


def onehot(rows, base, ids):
    at = lax.broadcasted_iota(jnp.int32, (rows, ids.shape[1]), 0) + base
    return jnp.where(at == ids, 1.0, 0.0).astype(BF16)


def bucket_kernel(
    pack_ref, src_ref, dst_ref, rel_ref, gs_out, gd_out, gr_out,
    acc_s, acc_d, acc_r, ohs, ohr, mm, cnt, dnat, relt,
):
    width, rows = src_ref.shape
    half = width // 2
    rels = rel_ref.shape[0]
    wide = relt.shape[1]
    blocks = TILES // 2
    acc_s[...] = jnp.zeros_like(acc_s)
    acc_d[...] = jnp.zeros_like(acc_d)
    acc_r[...] = jnp.zeros_like(acc_r)
    relt[...] = jnp.zeros_like(relt)
    eye = onehot(CHUNK, 0, lax.broadcasted_iota(jnp.int32, (1, CHUNK), 1))
    for c in range(rows // CHUNK):
        cut = pl.ds(c * CHUNK, CHUNK)
        turned = lax.dot_general(eye, dst_ref[:, cut], NT, preferred_element_type=F32)
        dnat[cut, :] = turned.astype(BF16)
    eye = onehot(width, 0, lax.broadcasted_iota(jnp.int32, (1, width), 1))
    for start in range(0, rels, CHUNK):
        cut = pl.ds(start, min(CHUNK, rels - start))
        turned = lax.dot_general(eye, rel_ref[cut, :].astype(BF16), NT, preferred_element_type=F32)
        relt[:, cut] = turned.astype(BF16)
    for k in range(blocks):
        total = 0.0
        for h in range(2):
            ids = pack_ref[pl.ds(3 * TILES + 2 * k + h, 1), :]
            low = onehot(128, 0, jnp.where(ids < 0, -1, ids & 127))
            high = onehot(rows // 128, 0, jnp.where(ids < 0, -1, ids >> 7))
            total = total + lax.dot_general(low, high, NT, preferred_element_type=F32)
        cnt[k] = total * (1.0 / (2 * LIVE))

    def tile(t, _):
        sid = pack_ref[pl.ds(t, 1), :]
        rid = pack_ref[pl.ds(TILES + t, 1), :]
        did = pack_ref[pl.ds(2 * TILES + t, 1), :]
        for c in range(rows // CHUNK):
            ohs[pl.ds(c * CHUNK, CHUNK), :] = onehot(CHUNK, c * CHUNK, sid)
        ohr[...] = onehot(wide, 0, rid)
        alive = jnp.where(did >= 0, 0.5, 0.0)
        s = jnp.dot(src_ref[...], ohs[...], preferred_element_type=F32)
        r = jnp.dot(relt[...], ohr[...], preferred_element_type=F32)
        sre, sim, rre, rim = s[:half], s[half:], r[:half], r[half:]
        rot = jnp.concatenate([sre * rre - sim * rim, sre * rim + sim * rre], 0)
        rot = (rot * alive).astype(BF16)
        weight = cnt[t // 2]
        for c in range(rows // CHUNK):
            cut = pl.ds(c * CHUNK, CHUNK)
            lean = jnp.tanh(jnp.dot(dnat[cut, :], rot, preferred_element_type=F32))
            share = jnp.concatenate([weight[:, 2 * c : 2 * c + 1], weight[:, 2 * c + 1 : 2 * c + 2]], 0)
            hit = lax.broadcasted_iota(jnp.int32, (CHUNK, TILE), 0) + c * CHUNK == did
            slope = jnp.where(hit, share + 1, share)
            mm[cut, :] = (slope * lean + jnp.where(hit, share - 1, share)).astype(BF16)
        g = jnp.dot(dst_ref[...], mm[...], preferred_element_type=F32) * alive
        acc_d[...] += lax.dot_general(rot, mm[...], NT, preferred_element_type=F32)
        gre, gim = g[:half], g[half:]
        gs = jnp.concatenate([gre * rre + gim * rim, gim * rre - gre * rim], 0).astype(BF16)
        gr = jnp.concatenate([gre * sre + gim * sim, gim * sre - gre * sim], 0).astype(BF16)
        acc_s[...] += lax.dot_general(gs, ohs[...], NT, preferred_element_type=F32)
        acc_r[pl.ds(0, wide), :] += lax.dot_general(ohr[...], gr, NT, preferred_element_type=F32)
        return 0

    lax.fori_loop(0, jnp.max(pack_ref[pl.ds(4 * TILES, TILES), :]), tile, 0)
    gs_out[...] = acc_s[...].astype(BF16)
    gd_out[...] = acc_d[...].astype(BF16)
    gr_out[...] = acc_r[...].astype(BF16)


def bucket(pack, src, dst, rel):
    width, rows = src.shape
    wide = -(-rel.shape[0] // 128) * 128
    vm = pl.BlockSpec(memory_space=pltpu.VMEM)
    return pl.pallas_call(
        bucket_kernel,
        out_shape=[
            jax.ShapeDtypeStruct((width, rows), BF16),
            jax.ShapeDtypeStruct((width, rows), BF16),
            jax.ShapeDtypeStruct((REL_ROWS, width), BF16),
        ],
        in_specs=[vm] * 4,
        out_specs=[vm] * 3,
        scratch_shapes=[
            pltpu.VMEM((width, rows), F32),
            pltpu.VMEM((width, rows), F32),
            pltpu.VMEM((REL_ROWS, width), F32),
            pltpu.VMEM((rows, TILE), BF16),
            pltpu.VMEM((wide, TILE), BF16),
            pltpu.VMEM((rows, TILE), BF16),
            pltpu.VMEM((TILES // 2, 128, rows // 128), F32),
            pltpu.VMEM((rows, width), BF16),
            pltpu.VMEM((width, wide), BF16),
        ],
        compiler_params=pltpu.CompilerParams(vmem_limit_bytes=VMEM_BYTES),
    )(pack, src, dst, rel)


class Group:
    def __init__(self, axis, size, sends, recvs):
        self.axis, self.size, self.sends, self.recvs = axis, size, sends, recvs
        self.me = lax.axis_index(axis)

    def copy(self, source, target, peer, slot):
        return pltpu.make_async_remote_copy(
            src_ref=source,
            dst_ref=target,
            send_sem=self.sends.at[peer],
            recv_sem=self.recvs.at[slot],
            device_id={self.axis: peer},
            device_id_type=MESH,
        )

    def others(self, act):
        def step(d, _):
            act(lax.rem(self.me + d, self.size))
            return 0

        lax.fori_loop(1, self.size, step, 0)

    def scatter(self, piece, slot):
        self.others(lambda p: self.copy(piece(p), slot(self.me), p, self.me).start())

    def landed(self, piece, slot):
        self.others(lambda p: self.copy(piece(p), slot(p), p, p).wait_recv())

    def sent(self, piece, slot):
        self.others(lambda p: self.copy(piece(p), slot(self.me), p, self.me).wait_send())


def meet():
    barrier = pltpu.get_barrier_semaphore()
    for axis, size in (("row", N_ROW), ("col", N_COL)):
        me = lax.axis_index(axis)

        def greet(d, _):
            peer = lax.rem(me + d, size)
            pl.semaphore_signal(barrier, inc=1, device_id={axis: peer}, device_id_type=MESH)
            return 0

        lax.fori_loop(1, size, greet, 0)
    pl.semaphore_wait(barrier, N_ROW + N_COL - 2)


def lanes(ref, width):
    return lambda i: ref.at[:, pl.ds(pl.multiple_of(i * width, width), width)]


def cuts(ref, height):
    return lambda i: ref.at[pl.ds(pl.multiple_of(i * height, height), height), :]


def own(ref):
    return lambda i: ref


def gather_kernel(src_ref, dst_ref, pack_ref, src_all, dst_all, pack_out, s1, r1, s2, r2, s3, r3):
    meet()
    cols = Group("col", N_COL, s1, r1)
    rows = Group("row", N_ROW, s2, r2)
    src_to = lanes(src_all, src_ref.shape[1])
    dst_to = lanes(dst_all, dst_ref.shape[1])
    partner = lax.rem(cols.me + HALF_COL, N_COL)
    rows.scatter(own(dst_ref), dst_to)
    cols.scatter(own(src_ref), src_to)
    swap = pltpu.make_async_remote_copy(
        src_ref=pack_ref,
        dst_ref=pack_out,
        send_sem=s3,
        recv_sem=r3,
        device_id={"col": partner},
        device_id_type=MESH,
    )
    swap.start()
    src_to(cols.me)[...] = src_ref[...]
    dst_to(rows.me)[...] = dst_ref[...]
    cols.landed(own(src_ref), src_to)
    rows.landed(own(dst_ref), dst_to)
    cols.sent(own(src_ref), src_to)
    rows.sent(own(dst_ref), dst_to)
    swap.wait()


def gather(src, dst, pack):
    vm = pl.BlockSpec(memory_space=pltpu.VMEM)
    sem = pltpu.SemaphoreType.DMA
    return pl.pallas_call(
        gather_kernel,
        out_shape=[
            jax.ShapeDtypeStruct((src.shape[0], src.shape[1] * N_COL), BF16),
            jax.ShapeDtypeStruct((dst.shape[0], dst.shape[1] * N_ROW), BF16),
            jax.ShapeDtypeStruct(pack.shape, pack.dtype),
        ],
        in_specs=[vm] * 3,
        out_specs=[vm] * 3,
        scratch_shapes=[sem((N_COL,)), sem((N_COL,)), sem((N_ROW,)), sem((N_ROW,)), sem, sem],
        compiler_params=pltpu.CompilerParams(
            collective_id=0, has_side_effects=True, vmem_limit_bytes=VMEM_BYTES
        ),
    )(src, dst, pack)


def total_of(land, size):
    total = land[0].astype(F32)
    for i in range(1, size):
        total = total + land[i].astype(F32)
    return total


def exchange_kernel(again, *refs):
    gs, gd, gr, src_ref, dst_ref = refs[:5]
    if again:
        rel_ref, his_ref, src_new, dst_new, src_all, dst_all, rel_new, his_new, g_all = refs[5:14]
        rest = refs[14:]
    else:
        src_new, dst_new, g_all = refs[5:8]
        rest = refs[8:]
    land_s, land_d, land_r, land_q = rest[:4]
    sems = rest[4:]
    meet()
    cut_s, cut_d = src_ref.shape[1], dst_ref.shape[1]
    first = Group("col", N_COL, sems[0], sems[1])
    src_sum = Group("col", N_COL, sems[2], sems[3])
    dst_sum = Group("row", N_ROW, sems[4], sems[5])
    second = Group("row", N_ROW, sems[6], sems[7])
    third = Group("col", N_COL, sems[8], sems[9])
    me_c, me_r = first.me, second.me
    slot_s, slot_d, slot_r, slot_q = land_s.at.__getitem__, land_d.at.__getitem__, land_r.at.__getitem__, land_q.at.__getitem__
    gr_cut, g_cut = cuts(gr, REL_CUT), cuts(g_all, REL_CUT)
    gs_cut, gd_cut = lanes(gs, cut_s), lanes(gd, cut_d)

    first.scatter(gr_cut, slot_r)
    dst_sum.scatter(gd_cut, slot_d)
    src_sum.scatter(gs_cut, slot_s)
    land_r[me_c] = gr_cut(me_c)[...]
    land_s[me_c] = gs_cut(me_c)[...]
    land_d[me_r] = gd_cut(me_r)[...]

    first.landed(gr_cut, slot_r)
    land_q[me_r] = total_of(land_r, N_COL).astype(BF16)
    second.scatter(lambda p: slot_q(me_r), slot_q)

    src_sum.landed(gs_cut, slot_s)
    share = src_ref[...].astype(F32) - entity_rate * total_of(land_s, N_COL)
    src_new[...] = share.astype(BF16)
    if again:
        src_to = lanes(src_all, cut_s)
        src_gather = Group("col", N_COL, sems[10], sems[11])
        src_gather.scatter(own(src_new), src_to)
        src_to(me_c)[...] = src_new[...]

    second.landed(lambda p: slot_q(me_r), slot_q)
    g_cut(me_c)[...] = total_of(land_q, N_ROW).astype(BF16)
    third.scatter(lambda p: g_cut(me_c), g_cut)

    dst_sum.landed(gd_cut, slot_d)
    share = dst_ref[...].astype(F32) - entity_rate * total_of(land_d, N_ROW)
    dst_new[...] = share.astype(BF16)
    if again:
        dst_to = lanes(dst_all, cut_d)
        dst_gather = Group("row", N_ROW, sems[12], sems[13])
        dst_gather.scatter(own(dst_new), dst_to)
        dst_to(me_r)[...] = dst_new[...]

    third.landed(lambda p: g_cut(me_c), g_cut)
    if again:
        rels = rel_ref.shape[0]
        for start in range(0, rels, CHUNK):
            at = pl.ds(start, min(CHUNK, rels - start))
            grads = g_all[at, :].astype(F32)
            history = his_ref[at, :] + grads * grads
            his_new[at, :] = history
            rel_new[at, :] = rel_ref[at, :] - relation_rate * grads / jnp.sqrt(history)
        src_gather.landed(own(src_new), src_to)
        dst_gather.landed(own(dst_new), dst_to)
        src_gather.sent(own(src_new), src_to)
        dst_gather.sent(own(dst_new), dst_to)
    first.sent(gr_cut, slot_r)
    src_sum.sent(gs_cut, slot_s)
    dst_sum.sent(gd_cut, slot_d)
    second.sent(lambda p: slot_q(me_r), slot_q)
    third.sent(lambda p: g_cut(me_c), g_cut)


def exchange(again, gs, gd, gr, src, dst, *relation):
    width = src.shape[0]
    vm = pl.BlockSpec(memory_space=pltpu.VMEM)
    sem = pltpu.SemaphoreType.DMA
    out_shape = [jax.ShapeDtypeStruct(src.shape, BF16), jax.ShapeDtypeStruct(dst.shape, BF16)]
    sizes = [N_COL, N_COL, N_COL, N_COL, N_ROW, N_ROW, N_ROW, N_ROW, N_COL, N_COL]
    if again:
        out_shape += [jax.ShapeDtypeStruct(gs.shape, BF16), jax.ShapeDtypeStruct(gd.shape, BF16)]
        out_shape += [jax.ShapeDtypeStruct(relation[0].shape, F32)] * 2
        sizes += [N_COL, N_COL, N_ROW, N_ROW]
    out_shape += [jax.ShapeDtypeStruct(gr.shape, BF16)]
    operands = (gs, gd, gr, src, dst, *relation)
    return pl.pallas_call(
        functools.partial(exchange_kernel, again),
        out_shape=out_shape,
        in_specs=[vm] * len(operands),
        out_specs=[vm] * len(out_shape),
        scratch_shapes=[
            pltpu.VMEM((N_COL, width, src.shape[1]), BF16),
            pltpu.VMEM((N_ROW, width, dst.shape[1]), BF16),
            pltpu.VMEM((N_COL, REL_CUT, width), BF16),
            pltpu.VMEM((N_ROW, REL_CUT, width), BF16),
        ]
        + [sem((n,)) for n in sizes],
        compiler_params=pltpu.CompilerParams(
            collective_id=1 if again else 2, has_side_effects=True, vmem_limit_bytes=VMEM_BYTES
        ),
    )(*operands)


def packed(src_ids, rel_ids, dst_ids, neg_ids, count):
    def rows_of(ids):
        return jnp.pad(ids.reshape(TILES, LIVE), ((0, 0), (0, TILE - LIVE)), constant_values=-1)

    live = jnp.arange(TILES * LIVE, dtype=jnp.int32) < count
    busy = jnp.broadcast_to((count + LIVE - 1) // LIVE, (TILES, TILE)).astype(jnp.int32)
    lists = [src_ids, rel_ids, jnp.where(live, dst_ids, -1), neg_ids.reshape(-1)]
    return jnp.concatenate([rows_of(ids) for ids in lists] + [busy], 0)


def on_device(
    source_table, dest_table, relations, rel_history, src_ids, rel_ids, dst_ids, neg_ids, counts
):
    src, dst = source_table[0].T, dest_table[0].T
    here, away = (
        packed(src_ids[0, 0, t], rel_ids[0, 0, t], dst_ids[0, 0, t], neg_ids[0, 0, t], counts[0, 0, t])
        for t in range(2)
    )
    src_all, dst_all, away = gather(src, dst, away)
    gs, gd, gr = bucket(here, src_all, dst_all, relations)
    src, dst, src_all, dst_all, relations, rel_history, _ = exchange(
        True, gs, gd, gr, src, dst, relations, rel_history
    )
    gs, gd, gr = bucket(away, src_all, dst_all, relations)
    src, dst, grads = exchange(False, gs, gd, gr, src, dst)
    grads = grads[: relations.shape[0]].astype(F32)
    history = rel_history + grads * grads
    relations = relations - relation_rate * grads / jnp.sqrt(history)
    return (src.T[None], dst.T[None], relations, history)


def solution(mesh):
    placed = (
        P("row", "col", None),
        P("col", "row", None),
        P(),
        P(),
        P("row", "col", None, None),
        P("row", "col", None, None),
        P("row", "col", None, None),
        P("row", "col", None, None, None),
        P("row", "col", None),
    )
    return jax.shard_map(
        on_device,
        mesh=mesh,
        in_specs=placed,
        out_specs=(P("row", "col", None), P("col", "row", None), P(), P()),
        check_vma=False,
    )
```

```python
import functools
import jax
import jax.numpy as jnp
from jax import lax
from jax.experimental import pallas as pl
from jax.experimental.pallas import tpu as pltpu
from jax.sharding import PartitionSpec as P

F32, BF16 = jnp.float32, jnp.bfloat16
MESH = pl.DeviceIdType.MESH
NT = (((1,), (1,)), ((), ()))
entity_rate = 0.3
relation_rate = 0.5
N_X, N_Y = 4, 4
N_ROW, N_COL = 8, 16
HALF_COL = 8
TILE, LIVE = 512, 500
TILES = 8
CHUNK = 256
REL_HALF, REL_CUT, REL_PIECE = 208, 384, 16
REL_ROWS, REL_WIDE = 2 * REL_HALF, N_X * REL_CUT
PIECES = REL_HALF // REL_PIECE
VMEM_BYTES = 60 * 2**20


def onehot(rows, base, ids):
    at = lax.broadcasted_iota(jnp.int32, (rows, ids.shape[1]), 0) + base
    return jnp.where(at == ids, 1.0, 0.0).astype(BF16)


def bucket_kernel(
    turn, sid_ref, rid_ref, did_ref, nid_ref, count_ref, src_ref, dst_ref, rel_ref,
    gs_out, gd_out, gr_out, acc_s, acc_d, acc_r, ohs, ohr, mm, cnt, dnat, relt, lists,
):
    width, rows = src_ref.shape
    half = width // 2
    blocks = TILES // 2
    count = jnp.max(count_ref[pl.ds(turn, 1), :])
    acc_s[...] = jnp.zeros_like(acc_s)
    acc_d[...] = jnp.zeros_like(acc_d)
    acc_r[...] = jnp.zeros_like(acc_r)
    relt[...] = jnp.zeros_like(relt)
    relt[:, pl.ds(0, rel_ref.shape[1])] = rel_ref[...].astype(BF16)
    eye = onehot(CHUNK, 0, lax.broadcasted_iota(jnp.int32, (1, CHUNK), 1))
    for c in range(rows // CHUNK):
        cut = pl.ds(c * CHUNK, CHUNK)
        turned = lax.dot_general(eye, dst_ref[:, cut], NT, preferred_element_type=F32)
        dnat[cut, :] = turned.astype(BF16)
    lists[...] = jnp.full(lists.shape, -1, jnp.int32)
    lane = lax.broadcasted_iota(jnp.int32, (1, LIVE), 1)
    for t in range(TILES):
        own = pl.ds(t * LIVE, LIVE)
        lists[0, pl.ds(t, 1), pl.ds(0, LIVE)] = sid_ref[pl.ds(turn, 1), own]
        lists[1, pl.ds(t, 1), pl.ds(0, LIVE)] = rid_ref[pl.ds(turn, 1), own]
        live = lane + t * LIVE < count
        lists[2, pl.ds(t, 1), pl.ds(0, LIVE)] = jnp.where(live, did_ref[pl.ds(turn, 1), own], -1)
    for k in range(blocks):
        ids = nid_ref[pl.ds(turn * blocks + k, 1), :]
        low = onehot(128, 0, ids & 127)
        high = onehot(rows // 128, 0, ids >> 7)
        total = lax.dot_general(low, high, NT, preferred_element_type=F32)
        cnt[k] = total * (1.0 / (2 * LIVE))

    def tile(t, _):
        sid, rid, did = (lists[i, pl.ds(t, 1), :] for i in range(3))
        for c in range(rows // CHUNK):
            ohs[pl.ds(c * CHUNK, CHUNK), :] = onehot(CHUNK, c * CHUNK, sid)
        ohr[...] = onehot(REL_WIDE, 0, rid)
        alive = jnp.where(did >= 0, 0.5, 0.0)
        s = jnp.dot(src_ref[...], ohs[...], preferred_element_type=F32)
        r = jnp.dot(relt[...], ohr[...], preferred_element_type=F32)
        sre, sim, rre, rim = s[:half], s[half:], r[:half], r[half:]
        rot = jnp.concatenate([sre * rre - sim * rim, sre * rim + sim * rre], 0)
        rot = (rot * alive).astype(BF16)
        weight = cnt[t // 2]
        for c in range(rows // CHUNK):
            cut = pl.ds(c * CHUNK, CHUNK)
            lean = jnp.tanh(jnp.dot(dnat[cut, :], rot, preferred_element_type=F32))
            share = jnp.concatenate([weight[:, 2 * c : 2 * c + 1], weight[:, 2 * c + 1 : 2 * c + 2]], 0)
            hit = lax.broadcasted_iota(jnp.int32, (CHUNK, TILE), 0) + c * CHUNK == did
            slope = jnp.where(hit, share + 1, share)
            mm[cut, :] = (slope * lean + jnp.where(hit, share - 1, share)).astype(BF16)
        g = jnp.dot(dst_ref[...], mm[...], preferred_element_type=F32) * alive
        acc_d[...] += lax.dot_general(rot, mm[...], NT, preferred_element_type=F32)
        gre, gim = g[:half], g[half:]
        gs = jnp.concatenate([gre * rre + gim * rim, gim * rre - gre * rim], 0).astype(BF16)
        gr = jnp.concatenate([gre * sre + gim * sim, gim * sre - gre * sim], 0).astype(BF16)
        acc_s[...] += lax.dot_general(gs, ohs[...], NT, preferred_element_type=F32)
        acc_r[...] += lax.dot_general(gr, ohr[...], NT, preferred_element_type=F32)
        return 0

    lax.fori_loop(0, (count + LIVE - 1) // LIVE, tile, 0)
    gs_out[...] = acc_s[...].astype(BF16)
    gd_out[...] = acc_d[...].astype(BF16)
    gr_out[pl.ds(0, width), :] = acc_r[...].astype(BF16)
    gr_out[pl.ds(width, REL_ROWS - width), :] = jnp.zeros((REL_ROWS - width, REL_WIDE), BF16)


def bucket(turn, lists, src, dst, rel):
    width, rows = src.shape
    vm = pl.BlockSpec(memory_space=pltpu.VMEM)
    return pl.pallas_call(
        functools.partial(bucket_kernel, turn),
        out_shape=[
            jax.ShapeDtypeStruct((width, rows), BF16),
            jax.ShapeDtypeStruct((width, rows), BF16),
            jax.ShapeDtypeStruct((REL_ROWS, REL_WIDE), BF16),
        ],
        in_specs=[vm] * 8,
        out_specs=[vm] * 3,
        scratch_shapes=[
            pltpu.VMEM((width, rows), F32),
            pltpu.VMEM((width, rows), F32),
            pltpu.VMEM((width, REL_WIDE), F32),
            pltpu.VMEM((rows, TILE), BF16),
            pltpu.VMEM((REL_WIDE, TILE), BF16),
            pltpu.VMEM((rows, TILE), BF16),
            pltpu.VMEM((TILES // 2, 128, rows // 128), F32),
            pltpu.VMEM((rows, width), BF16),
            pltpu.VMEM((width, REL_WIDE), BF16),
            pltpu.VMEM((3, TILES, TILE), jnp.int32),
        ],
        compiler_params=pltpu.CompilerParams(vmem_limit_bytes=VMEM_BYTES),
    )(*lists, src, dst, rel)


class Place:
    def __init__(self):
        self.row, self.col = lax.axis_index("row"), lax.axis_index("col")
        self.core = lax.rem(self.col, 2)
        self.x, self.y = lax.div(self.col, 4), lax.div(self.row, 2)
        self.z_hi = lax.rem(self.row, 2)
        self.xz = lax.div(self.col, 2)
        self.yz = self.row * 2 + lax.rem(self.xz, 2)

    def sibling(self, p=None):
        return {"row": self.row, "col": self.col + 1 - 2 * self.core}

    def at_x(self, p):
        return {"row": self.row, "col": 4 * p + lax.rem(self.col, 4)}

    def at_xz(self, p):
        return {"row": self.row, "col": 2 * p + self.core}

    def at_y(self, p):
        return {"row": 2 * p + self.z_hi, "col": self.col}

    def across(self, p=None):
        return {"row": self.row + 1 - 2 * self.z_hi, "col": self.col}

    def at_yz(self, p):
        return {"row": lax.div(p, 2), "col": 4 * self.x + 2 * lax.rem(p, 2) + self.core}

    def partner(self, p=None):
        return {"row": self.row, "col": lax.rem(self.col + HALF_COL, N_COL)}


def others(me, size, act):
    def step(d, _):
        act(lax.rem(me + d, size))
        return 0

    lax.fori_loop(1, size, step, 0)


def every(size, act):
    def step(d, _):
        act(d)
        return 0

    lax.fori_loop(0, size, step, 0)


def send(source, target, sems, peer, slot, device):
    return pltpu.make_async_remote_copy(
        src_ref=source,
        dst_ref=target,
        send_sem=sems[0].at[peer],
        recv_sem=sems[1].at[slot],
        device_id=device,
        device_id_type=MESH,
    )


def meet(here, groups):
    barrier = pltpu.get_barrier_semaphore()
    for me, size, where in groups:
        others(me, size, lambda p: pl.semaphore_signal(barrier, inc=1, device_id=where(p), device_id_type=MESH))
    pl.semaphore_wait(barrier, sum(size - 1 for _, size, _ in groups))


def lanes(ref, width):
    return lambda i: ref.at[:, pl.ds(pl.multiple_of(i * width, width), width)]


class SourceGather:
    def __init__(self, here, mine, table, sems):
        self.here, self.mine, self.to = here, mine, lanes(table, mine.shape[1])
        self.far, self.near = sems[:2], sems[2:]
        self.slot = lambda p: self.to(2 * p + here.core)
        self.back = lambda p: self.to(2 * p + 1 - here.core)

    def far_copy(self, source, target, p, slot):
        return send(source, target, self.far, p, slot, self.here.at_xz(p))

    def near_copy(self, source, target, p):
        return send(source, target, self.near, p, p, self.here.sibling())

    def start(self):
        me = self.here.xz
        others(me, N_ROW, lambda p: self.far_copy(self.mine, self.slot(me), p, me).start())
        self.near_copy(self.mine, self.slot(me), me).start()
        self.slot(me)[...] = self.mine[...]

    def forward(self):
        def step(p):
            self.far_copy(self.mine, self.slot(p), p, p).wait_recv()
            self.near_copy(self.slot(p), self.slot(p), p).start()

        others(self.here.xz, N_ROW, step)

    def finish(self):
        me = self.here.xz
        every(N_ROW, lambda p: self.near_copy(self.mine, self.back(p), p).wait_recv())
        others(me, N_ROW, lambda p: self.far_copy(self.mine, self.slot(me), p, me).wait_send())
        every(N_ROW, lambda p: self.near_copy(self.mine, self.slot(p), p).wait_send())


class DestGather:
    def __init__(self, here, mine, table, sems):
        self.here, self.mine, self.to = here, mine, lanes(table, mine.shape[1])
        self.pair, self.first, self.second = sems[:2], sems[2:4], sems[4:]
        self.slot = lambda p: self.to(2 * p + here.z_hi)
        self.back = lambda p: self.to(2 * p + 1 - here.z_hi)

    def pair_copy(self, target):
        return send(self.mine, target, self.pair, 0, 0, self.here.across())

    def copy(self, sems, source, target, p, slot):
        return send(source, target, sems, p, slot, self.here.at_y(p))

    def start(self):
        me = self.here.y
        self.pair_copy(self.slot(me)).start()
        others(me, N_Y, lambda p: self.copy(self.first, self.mine, self.slot(me), p, me).start())
        self.slot(me)[...] = self.mine[...]

    def forward(self):
        me = self.here.y
        got = self.back(me)
        self.pair_copy(got).wait_recv()
        others(me, N_Y, lambda p: self.copy(self.second, got, got, p, me).start())

    def finish(self):
        me = self.here.y
        others(me, N_Y, lambda p: self.copy(self.first, self.mine, self.slot(p), p, p).wait_recv())
        others(me, N_Y, lambda p: self.copy(self.second, self.mine, self.back(p), p, p).wait_recv())
        self.pair_copy(self.slot(me)).wait_send()
        others(me, N_Y, lambda p: self.copy(self.first, self.mine, self.slot(me), p, me).wait_send())
        others(me, N_Y, lambda p: self.copy(self.second, self.mine, self.back(me), p, me).wait_send())


GATHER_SEMS = [N_ROW] * 4 + [1, 1] + [N_Y] * 4


def gather_kernel(src_ref, dst_ref, *refs):
    lists, (src_all, dst_all), swapped = refs[:5], refs[5:7], refs[7:12]
    sems = refs[12:]
    here = Place()
    meet(
        here,
        [
            (here.core, 2, here.sibling),
            (here.xz, N_ROW, here.at_xz),
            (here.y, N_Y, here.at_y),
            (here.z_hi, 2, here.across),
        ],
    )
    dst = DestGather(here, dst_ref, dst_all, sems[6:12])
    src = SourceGather(here, src_ref, src_all, sems[2:6])
    dst.start()
    src.start()
    swaps = [send(a, b, sems[:2], i, i, here.partner()) for i, (a, b) in enumerate(zip(lists, swapped))]
    for swap in swaps:
        swap.start()
    dst.forward()
    src.forward()
    dst.finish()
    src.finish()
    for swap in swaps:
        swap.wait()


def gather(src, dst, lists):
    vm = pl.BlockSpec(memory_space=pltpu.VMEM)
    sem = pltpu.SemaphoreType.DMA
    return pl.pallas_call(
        gather_kernel,
        out_shape=[
            jax.ShapeDtypeStruct((src.shape[0], src.shape[1] * N_COL), BF16),
            jax.ShapeDtypeStruct((dst.shape[0], dst.shape[1] * N_ROW), BF16),
        ]
        + [jax.ShapeDtypeStruct(a.shape, a.dtype) for a in lists],
        in_specs=[vm] * 7,
        out_specs=[vm] * 7,
        scratch_shapes=[sem((n,)) for n in [len(lists)] * 2 + GATHER_SEMS],
        compiler_params=pltpu.CompilerParams(
            collective_id=0, has_side_effects=True, vmem_limit_bytes=VMEM_BYTES
        ),
    )(src, dst, *lists)


def total_of(land, size):
    total = land[0].astype(F32)
    for i in range(1, size):
        total = total + land[i].astype(F32)
    return total


def exchange_kernel(again, *refs):
    gs, gd, gr, src_ref, dst_ref = refs[:5]
    if again:
        rel_ref, his_ref, src_new, dst_new, g_all, src_all, dst_all, rel_new, his_new = refs[5:14]
        rest = refs[14:]
    else:
        src_new, dst_new, g_all = refs[5:8]
        rest = refs[8:]
    s_near, s_part, s_far, d_across, d_own, d_part, d_last, r_near, r_part, r_far, r_chunk, r_land = rest[:12]
    sems = rest[12:]
    here = Place()
    me_x, me_y, me_u, me_q = here.x, here.y, here.xz, here.yz
    meet(
        here,
        [
            (here.core, 2, here.sibling),
            (here.xz, N_ROW, here.at_xz),
            (here.yz, N_COL, here.at_yz),
        ],
    )
    cut_s, cut_d = src_ref.shape[1], dst_ref.shape[1]
    gs_cut, gd_cut = lanes(gs, cut_s), lanes(gd, cut_d)

    def rel_cut(ref, core, x):
        down = pl.ds(pl.multiple_of(core * REL_HALF, REL_PIECE), REL_HALF)
        return ref.at[down, pl.ds(pl.multiple_of(x * REL_CUT, REL_CUT), REL_CUT)]

    def piece(ref, w, core, x):
        down = pl.ds(pl.multiple_of(core * REL_HALF + w * REL_PIECE, REL_PIECE), REL_PIECE)
        return ref.at[down, pl.ds(pl.multiple_of(x * REL_CUT, REL_CUT), REL_CUT)]

    def part(ref, w):
        return ref.at[pl.ds(pl.multiple_of(w * REL_PIECE, REL_PIECE), REL_PIECE), :]

    near_r = lambda x: send(rel_cut(gr, 1 - here.core, x), r_near.at[x], sems[0:2], x, x, here.sibling())
    far_r = lambda x, slot: send(r_part.at[x], r_far.at[slot], sems[2:4], x, slot, here.at_x(x))
    sum_r = lambda w, slot: send(part(r_chunk, w), r_land.at[slot], sems[4:6], w, slot, here.at_yz(w))
    back_r = lambda p, w: send(
        piece(g_all, w, here.core, me_x), piece(g_all, w, here.core, me_x), sems[6:8], p, w, here.at_yz(p)
    )
    wide_r = lambda p, x: send(
        rel_cut(g_all, here.core, x), rel_cut(g_all, here.core, x), sems[8:10], p, x, here.at_x(p)
    )
    last_r = lambda core, x: send(
        rel_cut(g_all, core, x), rel_cut(g_all, core, x), sems[10:12], x, x, here.sibling()
    )
    near_s = lambda u: send(gs_cut(2 * u + 1 - here.core), s_near.at[u], sems[12:14], u, u, here.sibling())
    far_s = lambda u, slot: send(s_part.at[u], s_far.at[slot], sems[14:16], u, slot, here.at_xz(u))
    far_a = lambda p, slot: send(
        gd_cut(2 * p + 1 - here.z_hi), d_across.at[slot], sems[16:18], p, slot, here.at_y(p)
    )
    far_o = lambda p, slot: send(gd_cut(2 * p + here.z_hi), d_own.at[slot], sems[18:20], p, slot, here.at_y(p))
    pair_d = send(d_part, d_last, sems[20:22], 0, 0, here.across())

    every(N_X, lambda x: near_r(x).start())
    others(me_y, N_Y, lambda p: far_a(p, me_y).start())
    others(me_y, N_Y, lambda p: far_o(p, me_y).start())
    every(N_ROW, lambda u: near_s(u).start())
    d_across[me_y] = gd_cut(2 * me_y + 1 - here.z_hi)[...]
    d_own[me_y] = gd_cut(2 * me_y + here.z_hi)[...]

    def relation_part(x):
        near_r(x).wait_recv()
        return (rel_cut(gr, here.core, x)[...].astype(F32) + r_near[x].astype(F32)).astype(BF16)

    def relation_send(x):
        r_part[x] = relation_part(x)
        far_r(x, me_x).start()

    others(me_x, N_X, relation_send)
    r_far[me_x] = relation_part(me_x)

    def source_part(u):
        near_s(u).wait_recv()
        return (gs_cut(2 * u + here.core)[...].astype(F32) + s_near[u].astype(F32)).astype(BF16)

    def source_send(u):
        s_part[u] = source_part(u)
        far_s(u, me_u).start()

    others(me_u, N_ROW, source_send)
    s_far[me_u] = source_part(me_u)

    others(me_x, N_X, lambda x: far_r(x, x).wait_recv())
    r_chunk[...] = total_of(r_far, N_X).astype(BF16)

    def piece_step(act):
        def step(w):
            @pl.when(w != me_q)
            def _():
                act(w)

        every(PIECES, step)

    piece_step(lambda w: sum_r(w, me_q).start())

    others(me_y, N_Y, lambda p: far_a(p, p).wait_recv())
    d_part[...] = total_of(d_across, N_Y).astype(BF16)
    pair_d.start()

    @pl.when(me_q < PIECES)
    def _():
        r_land[me_q] = part(r_chunk, me_q)[...]
        others(me_q, N_COL, lambda p: sum_r(me_q, p).wait_recv())
        piece(g_all, me_q, here.core, me_x)[...] = total_of(r_land, N_COL).astype(BF16)
        others(me_q, N_COL, lambda p: back_r(p, me_q).start())

    others(me_u, N_ROW, lambda u: far_s(u, u).wait_recv())
    share = src_ref[...].astype(F32) - entity_rate * total_of(s_far, N_ROW)
    src_new[...] = share.astype(BF16)
    if again:
        src_gather = SourceGather(here, src_new, src_all, sems[22:26])
        src_gather.start()

    others(me_y, N_Y, lambda p: far_o(p, p).wait_recv())
    pair_d.wait_recv()
    share = total_of(d_own, N_Y) + d_last[...].astype(F32)
    dst_new[...] = (dst_ref[...].astype(F32) - entity_rate * share).astype(BF16)
    if again:
        dst_gather = DestGather(here, dst_new, dst_all, sems[26:32])
        dst_gather.start()

    piece_step(lambda w: back_r(w, w).wait_recv())
    others(me_x, N_X, lambda p: wide_r(p, me_x).start())
    last_r(here.core, me_x).start()
    if again:
        dst_gather.forward()

    def relation_forward(x):
        wide_r(x, x).wait_recv()
        last_r(here.core, x).start()

    others(me_x, N_X, relation_forward)
    if again:
        src_gather.forward()
    every(N_X, lambda x: last_r(1 - here.core, x).wait_recv())
    if again:
        width, rels = rel_ref.shape
        for start in range(0, rels, CHUNK):
            at = pl.ds(start, min(CHUNK, rels - start))
            grads = g_all[pl.ds(0, width), at].astype(F32)
            history = his_ref[:, at] + grads * grads
            his_new[:, at] = history
            rel_new[:, at] = rel_ref[:, at] - relation_rate * grads / jnp.sqrt(history)
        src_gather.finish()
        dst_gather.finish()

    every(N_X, lambda x: near_r(x).wait_send())
    others(me_x, N_X, lambda x: far_r(x, me_x).wait_send())
    piece_step(lambda w: sum_r(w, me_q).wait_send())

    @pl.when(me_q < PIECES)
    def _():
        others(me_q, N_COL, lambda p: back_r(p, me_q).wait_send())

    others(me_x, N_X, lambda p: wide_r(p, me_x).wait_send())
    every(N_X, lambda x: last_r(here.core, x).wait_send())
    every(N_ROW, lambda u: near_s(u).wait_send())
    others(me_u, N_ROW, lambda u: far_s(u, me_u).wait_send())
    others(me_y, N_Y, lambda p: far_a(p, me_y).wait_send())
    others(me_y, N_Y, lambda p: far_o(p, me_y).wait_send())
    pair_d.wait_send()


def exchange(again, gs, gd, gr, src, dst, *relation):
    width, cut_s, cut_d = src.shape[0], src.shape[1], dst.shape[1]
    vm = pl.BlockSpec(memory_space=pltpu.VMEM)
    sem = pltpu.SemaphoreType.DMA
    out_shape = [jax.ShapeDtypeStruct(a.shape, BF16) for a in (src, dst, gr)]
    sizes = [N_X] * 4 + [N_COL] * 4 + [N_X] * 4 + [N_ROW] * 4 + [N_Y] * 4 + [1, 1]
    if again:
        out_shape += [jax.ShapeDtypeStruct(a.shape, a.dtype) for a in (gs, gd, *relation)]
        sizes += GATHER_SEMS
    operands = (gs, gd, gr, src, dst, *relation)
    return pl.pallas_call(
        functools.partial(exchange_kernel, again),
        out_shape=out_shape,
        in_specs=[vm] * len(operands),
        out_specs=[vm] * len(out_shape),
        scratch_shapes=[
            pltpu.VMEM((N_ROW, width, cut_s), BF16),
            pltpu.VMEM((N_ROW, width, cut_s), BF16),
            pltpu.VMEM((N_ROW, width, cut_s), BF16),
            pltpu.VMEM((N_Y, width, cut_d), BF16),
            pltpu.VMEM((N_Y, width, cut_d), BF16),
            pltpu.VMEM((width, cut_d), BF16),
            pltpu.VMEM((width, cut_d), BF16),
            pltpu.VMEM((N_X, REL_HALF, REL_CUT), BF16),
            pltpu.VMEM((N_X, REL_HALF, REL_CUT), BF16),
            pltpu.VMEM((N_X, REL_HALF, REL_CUT), BF16),
            pltpu.VMEM((REL_HALF, REL_CUT), BF16),
            pltpu.VMEM((N_COL, REL_PIECE, REL_CUT), BF16),
        ]
        + [sem((n,)) for n in sizes],
        compiler_params=pltpu.CompilerParams(
            collective_id=1 if again else 2, has_side_effects=True, vmem_limit_bytes=VMEM_BYTES
        ),
    )(*operands)


def on_device(
    source_table, dest_table, relations, rel_history, src_ids, rel_ids, dst_ids, neg_ids, counts
):
    src, dst = source_table[0].T, dest_table[0].T
    rel, history = relations.T, rel_history.T
    blocks, negs = neg_ids.shape[3:]
    count = jnp.broadcast_to(counts[0, 0][:, None], (2, 128))
    here = [src_ids[0, 0], rel_ids[0, 0], dst_ids[0, 0], neg_ids[0, 0].reshape(2 * blocks, negs), count]
    src_all, dst_all, *away = gather(src, dst, here)
    gs, gd, gr = bucket(0, here, src_all, dst_all, rel)
    src, dst, _, src_all, dst_all, rel, history = exchange(True, gs, gd, gr, src, dst, rel, history)
    gs, gd, gr = bucket(1, away, src_all, dst_all, rel)
    src, dst, grads = exchange(False, gs, gd, gr, src, dst)
    grads = grads[: rel.shape[0], : rel.shape[1]].astype(F32)
    history = history + grads * grads
    rel = rel - relation_rate * grads / jnp.sqrt(history)
    return (src.T[None], dst.T[None], rel.T, history.T)


def solution(mesh):
    placed = (
        P("row", "col", None),
        P("col", "row", None),
        P(),
        P(),
        P("row", "col", None, None),
        P("row", "col", None, None),
        P("row", "col", None, None),
        P("row", "col", None, None, None),
        P("row", "col", None),
    )
    return jax.shard_map(
        on_device,
        mesh=mesh,
        in_specs=placed,
        out_specs=(P("row", "col", None), P("col", "row", None), P(), P()),
        check_vma=False,
    )
```

```python
import functools
import jax
import jax.numpy as jnp
from jax import lax
from jax.experimental import pallas as pl
from jax.experimental.pallas import tpu as pltpu
from jax.sharding import PartitionSpec as P

F32, BF16 = jnp.float32, jnp.bfloat16
MESH = pl.DeviceIdType.MESH
NT = (((1,), (1,)), ((), ()))
entity_rate = 0.3
relation_rate = 0.5
N_X, N_Y = 4, 4
N_ROW, N_COL = 8, 16
HALF_COL = 8
TILE, LIVE = 512, 500
TILES = 8
CHUNK, PAIR = 256, 512
SLOTS = TILES * TILE
REL_HALF, REL_CUT, REL_PIECE = 208, 384, 16
REL_ROWS, REL_WIDE = 2 * REL_HALF, N_X * REL_CUT
PIECES = REL_HALF // REL_PIECE
VMEM_BYTES = 60 * 2**20


class Place:
    def __init__(self):
        self.row, self.col = lax.axis_index("row"), lax.axis_index("col")
        self.core = lax.rem(self.col, 2)
        self.x, self.y = lax.div(self.col, 4), lax.div(self.row, 2)
        self.z_hi = lax.rem(self.row, 2)
        self.xz = lax.div(self.col, 2)
        self.yz = self.row * 2 + lax.rem(self.xz, 2)

    def sibling(self, p=None):
        return {"row": self.row, "col": self.col + 1 - 2 * self.core}

    def at_x(self, p):
        return {"row": self.row, "col": 4 * p + lax.rem(self.col, 4)}

    def at_xz(self, p):
        return {"row": self.row, "col": 2 * p + self.core}

    def at_y(self, p):
        return {"row": 2 * p + self.z_hi, "col": self.col}

    def across(self, p=None):
        return {"row": self.row + 1 - 2 * self.z_hi, "col": self.col}

    def at_yz(self, p):
        return {"row": lax.div(p, 2), "col": 4 * self.x + 2 * lax.rem(p, 2) + self.core}

    def partner(self, p=None):
        return {"row": self.row, "col": lax.rem(self.col + HALF_COL, N_COL)}


def others(me, size, act):
    def step(d, _):
        act(lax.rem(me + d, size))
        return 0

    lax.fori_loop(1, size, step, 0)


def every(size, act):
    def step(d, _):
        act(d)
        return 0

    lax.fori_loop(0, size, step, 0)


def send(source, target, sems, peer, slot, device):
    return pltpu.make_async_remote_copy(
        src_ref=source,
        dst_ref=target,
        send_sem=sems[0].at[peer],
        recv_sem=sems[1].at[slot],
        device_id=device,
        device_id_type=MESH,
    )


def meet(here, groups):
    barrier = pltpu.get_barrier_semaphore()
    for me, size, where in groups:
        others(me, size, lambda p: pl.semaphore_signal(barrier, inc=1, device_id=where(p), device_id_type=MESH))
    pl.semaphore_wait(barrier, sum(size - 1 for _, size, _ in groups))


def lanes(ref, width):
    return lambda i: ref.at[:, pl.ds(pl.multiple_of(i * width, width), width)]


class SourceGather:
    def __init__(self, here, mine, table, sems):
        self.here, self.mine, self.to = here, mine, lanes(table, mine.shape[1])
        self.far, self.near = sems[:2], sems[2:]
        self.slot = lambda p: self.to(2 * p + here.core)
        self.back = lambda p: self.to(2 * p + 1 - here.core)

    def far_copy(self, source, target, p, slot):
        return send(source, target, self.far, p, slot, self.here.at_xz(p))

    def near_copy(self, source, target, p):
        return send(source, target, self.near, p, p, self.here.sibling())

    def start(self):
        me = self.here.xz
        others(me, N_ROW, lambda p: self.far_copy(self.mine, self.slot(me), p, me).start())
        self.near_copy(self.mine, self.slot(me), me).start()
        self.slot(me)[...] = self.mine[...]

    def forward(self):
        def step(p):
            self.far_copy(self.mine, self.slot(p), p, p).wait_recv()
            self.near_copy(self.slot(p), self.slot(p), p).start()

        others(self.here.xz, N_ROW, step)

    def arrive(self):
        every(N_ROW, lambda p: self.near_copy(self.mine, self.back(p), p).wait_recv())

    def drain(self):
        me = self.here.xz
        others(me, N_ROW, lambda p: self.far_copy(self.mine, self.slot(me), p, me).wait_send())
        every(N_ROW, lambda p: self.near_copy(self.mine, self.slot(p), p).wait_send())


class DestGather:
    def __init__(self, here, mine, table, sems):
        self.here, self.mine, self.to = here, mine, lanes(table, mine.shape[1])
        self.pair, self.first, self.second = sems[:2], sems[2:4], sems[4:]
        self.slot = lambda p: self.to(2 * p + here.z_hi)
        self.back = lambda p: self.to(2 * p + 1 - here.z_hi)

    def pair_copy(self, target):
        return send(self.mine, target, self.pair, 0, 0, self.here.across())

    def copy(self, sems, source, target, p, slot):
        return send(source, target, sems, p, slot, self.here.at_y(p))

    def start(self):
        me = self.here.y
        self.pair_copy(self.slot(me)).start()
        others(me, N_Y, lambda p: self.copy(self.first, self.mine, self.slot(me), p, me).start())
        self.slot(me)[...] = self.mine[...]

    def forward(self):
        me = self.here.y
        got = self.back(me)
        self.pair_copy(got).wait_recv()
        others(me, N_Y, lambda p: self.copy(self.second, got, got, p, me).start())

    def arrive(self, p):
        self.copy(self.first, self.mine, self.slot(p), p, p).wait_recv()
        self.copy(self.second, self.mine, self.back(p), p, p).wait_recv()

    def drain(self):
        me = self.here.y
        self.pair_copy(self.slot(me)).wait_send()
        others(me, N_Y, lambda p: self.copy(self.first, self.mine, self.slot(me), p, me).wait_send())
        others(me, N_Y, lambda p: self.copy(self.second, self.mine, self.back(me), p, me).wait_send())


def onehot(rows, base, ids):
    at = lax.broadcasted_iota(jnp.int32, (rows, ids.shape[1]), 0) + base
    return jnp.where(at == ids, 1.0, 0.0).astype(BF16)


def total_of(land, size):
    total = land[0].astype(F32)
    for i in range(1, size):
        total = total + land[i].astype(F32)
    return total


def tile_at(t, size=TILE):
    return pl.ds(pl.multiple_of(t * size, size), size)


SCRATCH = dict(
    src_all=lambda w: pltpu.VMEM((w, 2048), BF16),
    dst_all=lambda w: pltpu.VMEM((w, 2048), BF16),
    dnat=lambda w: pltpu.VMEM((PAIR, w), BF16),
    relt=lambda w: pltpu.VMEM((w, REL_WIDE), BF16),
    s_all=lambda w: pltpu.VMEM((TILES, 2, w // 2, TILE), BF16),
    r_all=lambda w: pltpu.VMEM((TILES, 2, w // 2, TILE), BF16),
    rot=lambda w: pltpu.VMEM((w, SLOTS), BF16),
    gr_all=lambda w: pltpu.VMEM((w, SLOTS), BF16),
    g=lambda w: pltpu.VMEM((w, SLOTS), F32),
    mm=lambda w: pltpu.VMEM((PAIR, SLOTS), BF16),
    cnt=lambda w: pltpu.VMEM((TILES // 2, 2048, 128), F32),
    ohs=lambda w: pltpu.VMEM((2048, TILE), BF16),
    ohr=lambda w: pltpu.VMEM((REL_WIDE, TILE), BF16),
    lists=lambda w: pltpu.VMEM((8, SLOTS), jnp.int32),
    gd=lambda w: pltpu.VMEM((w, 2048), BF16),
    gs=lambda w: pltpu.VMEM((w, 2048), BF16),
    gr=lambda w: pltpu.VMEM((REL_ROWS, REL_WIDE), BF16),
    g_all=lambda w: pltpu.VMEM((REL_ROWS, REL_WIDE), BF16),
    s_near=lambda w: pltpu.VMEM((N_ROW, w, 128), BF16),
    s_part=lambda w: pltpu.VMEM((N_ROW, w, 128), BF16),
    s_far=lambda w: pltpu.VMEM((N_ROW, w, 128), BF16),
    d_across=lambda w: pltpu.VMEM((N_Y, w, 256), BF16),
    d_own=lambda w: pltpu.VMEM((N_Y, w, 256), BF16),
    d_part=lambda w: pltpu.VMEM((w, 256), BF16),
    d_last=lambda w: pltpu.VMEM((w, 256), BF16),
    r_near=lambda w: pltpu.VMEM((N_X, REL_HALF, REL_CUT), BF16),
    r_part=lambda w: pltpu.VMEM((N_X, REL_HALF, REL_CUT), BF16),
    r_far=lambda w: pltpu.VMEM((N_X, REL_HALF, REL_CUT), BF16),
    r_chunk=lambda w: pltpu.VMEM((REL_HALF, REL_CUT), BF16),
    r_land=lambda w: pltpu.VMEM((N_COL, REL_PIECE, REL_CUT), BF16),
)
SEMS = dict(
    swap=5, near_r=N_X, far_r=N_X, sum_r=N_COL, back_r=N_COL, wide_r=N_X, last_r=N_X, near_s=N_ROW, far_s=N_ROW,
    far_a=N_Y, far_o=N_Y, pair_d=1, src_far=N_ROW, src_near=N_ROW, dst_pair=1, dst_first=N_Y, dst_second=N_Y,
)


class Refs:
    pass


def kernel(*refs):
    refs = list(refs)
    k = Refs()
    for name in ("src", "dst"):
        setattr(k, name, refs.pop(0))
    lists_here = [refs.pop(0) for _ in range(5)]
    rel_in, his_in = refs.pop(0), refs.pop(0)
    for name in ("src_new", "dst_new", "rel", "his"):
        setattr(k, name, refs.pop(0))
    lists_away = [refs.pop(0) for _ in range(5)]
    for name in SCRATCH:
        setattr(k, name, refs.pop(0))
    sems = {name: (refs.pop(0), refs.pop(0)) for name in SEMS}
    load_sems = refs.pop(0)
    width = k.src.shape[0]
    half = width // 2
    rels = rel_in.shape[1]
    here = Place()
    me_x, me_y, me_u, me_q = here.x, here.y, here.xz, here.yz

    loads = [pltpu.make_async_copy(a, b, load_sems.at[i]) for i, (a, b) in enumerate([(rel_in, k.rel), (his_in, k.his)])]
    for load in loads:
        load.start()
    meet(here, [(here.core, 2, here.sibling), (me_u, N_ROW, here.at_xz), (me_q, N_COL, here.at_yz)])
    gathers = []
    for src, dst in ((k.src, k.dst), (k.src_new, k.dst_new)):
        gathers.append((
            SourceGather(here, src, k.src_all, sems["src_far"] + sems["src_near"]),
            DestGather(here, dst, k.dst_all, sems["dst_pair"] + sems["dst_first"] + sems["dst_second"]),
        ))
    src_gather, dst_gather = gathers[0]
    dst_gather.start()
    src_gather.start()
    swaps = [send(a, b, sems["swap"], i, i, here.partner()) for i, (a, b) in enumerate(zip(lists_here, lists_away))]
    for swap in swaps:
        swap.start()


    gs_cut, gd_cut = lanes(k.gs, 128), lanes(k.gd, 256)

    def rel_cut(ref, core, x):
        down = pl.ds(pl.multiple_of(core * REL_HALF, REL_PIECE), REL_HALF)
        return ref.at[down, pl.ds(pl.multiple_of(x * REL_CUT, REL_CUT), REL_CUT)]

    def piece(ref, w, core, x):
        down = pl.ds(pl.multiple_of(core * REL_HALF + w * REL_PIECE, REL_PIECE), REL_PIECE)
        return ref.at[down, pl.ds(pl.multiple_of(x * REL_CUT, REL_CUT), REL_CUT)]

    def part(ref, w):
        return ref.at[pl.ds(pl.multiple_of(w * REL_PIECE, REL_PIECE), REL_PIECE), :]

    def same(ref, name, peer, slot, device):
        return send(ref, ref, sems[name], peer, slot, device)

    near_r = lambda x: send(rel_cut(k.gr, 1 - here.core, x), k.r_near.at[x], sems["near_r"], x, x, here.sibling())
    far_r = lambda x, slot: send(k.r_part.at[x], k.r_far.at[slot], sems["far_r"], x, slot, here.at_x(x))
    sum_r = lambda w, slot: send(part(k.r_chunk, w), k.r_land.at[slot], sems["sum_r"], w, slot, here.at_yz(w))
    back_r = lambda p, w: same(piece(k.g_all, w, here.core, me_x), "back_r", p, w, here.at_yz(p))
    wide_r = lambda p, x: same(rel_cut(k.g_all, here.core, x), "wide_r", p, x, here.at_x(p))
    last_r = lambda core, x: same(rel_cut(k.g_all, core, x), "last_r", x, x, here.sibling())
    near_s = lambda u: send(gs_cut(2 * u + 1 - here.core), k.s_near.at[u], sems["near_s"], u, u, here.sibling())
    far_s = lambda u, slot: send(k.s_part.at[u], k.s_far.at[slot], sems["far_s"], u, slot, here.at_xz(u))
    far_a = lambda p, slot: send(
        gd_cut(2 * p + 1 - here.z_hi), k.d_across.at[slot], sems["far_a"], p, slot, here.at_y(p)
    )
    far_o = lambda p, slot: send(gd_cut(2 * p + here.z_hi), k.d_own.at[slot], sems["far_o"], p, slot, here.at_y(p))
    pair_d = send(k.d_part, k.d_last, sems["pair_d"], 0, 0, here.across())

    def piece_step(act):
        def step(w):
            @pl.when(w != me_q)
            def _():
                act(w)

        every(PIECES, step)


    def read_lists(turn, sid, rid, did, nid, count):
        k.lists[...] = jnp.full(k.lists.shape, -1, jnp.int32)
        limit = count[pl.ds(turn, 1), pl.ds(0, LIVE)]
        lane = lax.broadcasted_iota(jnp.int32, (1, LIVE), 1)
        for t in range(TILES):
            own, to = pl.ds(t * LIVE, LIVE), pl.ds(t * TILE, LIVE)
            k.lists[pl.ds(0, 1), to] = sid[pl.ds(turn, 1), own]
            k.lists[pl.ds(1, 1), to] = rid[pl.ds(turn, 1), own]
            k.lists[pl.ds(2, 1), to] = jnp.where(lane + t * LIVE < limit, did[pl.ds(turn, 1), own], -1)
        blocks = TILES // 2
        for b in range(blocks):
            ids = nid[pl.ds(turn * blocks + b, 1), :]
            low = onehot(128, 0, ids & 127)
            high = onehot(16, 0, ids >> 7)
            total = lax.dot_general(low, high, NT, preferred_element_type=F32) * (1.0 / (2 * LIVE))
            for h in range(16):
                k.cnt[b, pl.ds(h * 128, 128), :] = jnp.broadcast_to(total[:, h : h + 1], (128, 128))

    def cast_relations():
        k.relt[...] = jnp.zeros_like(k.relt)
        k.relt[:, pl.ds(0, rels)] = k.rel[...].astype(BF16)

    def pick_relations():
        def step(t):
            k.ohr[...] = onehot(REL_WIDE, 0, k.lists[pl.ds(1, 1), tile_at(t)])
            r = jnp.dot(k.relt[...], k.ohr[...], preferred_element_type=F32).astype(BF16)
            k.r_all[t, 0] = r[:half]
            k.r_all[t, 1] = r[half:]

        every(TILES, step)

    def pick_sources():
        def step(t):
            sid = k.lists[pl.ds(0, 1), tile_at(t)]
            alive = jnp.where(k.lists[pl.ds(2, 1), tile_at(t)] >= 0, 0.5, 0.0)
            for c in range(2048 // CHUNK):
                k.ohs[pl.ds(c * CHUNK, CHUNK), :] = onehot(CHUNK, c * CHUNK, sid)
            s = jnp.dot(k.src_all[...], k.ohs[...], preferred_element_type=F32)
            sre, sim = s[:half], s[half:]
            rre, rim = k.r_all[t, 0].astype(F32), k.r_all[t, 1].astype(F32)
            k.s_all[t, 0] = sre.astype(BF16)
            k.s_all[t, 1] = sim.astype(BF16)
            rot = jnp.concatenate([sre * rre - sim * rim, sre * rim + sim * rre], 0)
            k.rot[:, tile_at(t)] = (rot * alive).astype(BF16)
            k.g[:, tile_at(t)] = jnp.zeros((width, TILE), F32)

        every(TILES, step)

    def score(dst_gather):
        eye = onehot(CHUNK, 0, lax.broadcasted_iota(jnp.int32, (1, CHUNK), 1))

        def pair_step(d):
            y = lax.rem(me_y + d, N_Y)

            @pl.when(d > 0)
            def _():
                dst_gather.arrive(y)

            for h in range(2):
                some = k.dst_all[:, pl.ds(pl.multiple_of(y * PAIR + h * CHUNK, CHUNK), CHUNK)]
                turned = lax.dot_general(eye, some, NT, preferred_element_type=F32)
                k.dnat[pl.ds(h * CHUNK, CHUNK), :] = turned.astype(BF16)

            def step(t):
                did = k.lists[pl.ds(2, 1), tile_at(t)]
                rot = k.rot[:, tile_at(t)]
                for h in range(2):
                    down = pl.ds(h * CHUNK, CHUNK)
                    base = y * PAIR + h * CHUNK
                    lean = jnp.tanh(jnp.dot(k.dnat[down, :], rot, preferred_element_type=F32))
                    share = k.cnt[lax.div(t, 2), pl.ds(pl.multiple_of(base, CHUNK), CHUNK), :]
                    share = jnp.concatenate([share] * (TILE // 128), 1)
                    hit = lax.broadcasted_iota(jnp.int32, (CHUNK, TILE), 0) + base == did
                    slope = jnp.where(hit, share + 1, share)
                    k.mm[down, tile_at(t)] = (slope * lean + jnp.where(hit, share - 1, share)).astype(BF16)
                k.g[:, tile_at(t)] += jnp.dot(
                    k.dst_all[:, tile_at(y, PAIR)], k.mm[:, tile_at(t)], preferred_element_type=F32
                )

            every(TILES, step)
            total = lax.dot_general(k.rot[...], k.mm[...], NT, preferred_element_type=F32)
            k.gd[:, tile_at(y, PAIR)] = total.astype(BF16)

            @pl.when(d > 0)
            def _():
                far_a(y, me_y).start()
                far_o(y, me_y).start()

        every(N_Y, pair_step)
        k.d_across[me_y] = gd_cut(2 * me_y + 1 - here.z_hi)[...]
        k.d_own[me_y] = gd_cut(2 * me_y + here.z_hi)[...]

    def edge_grads():
        def step(t):
            alive = jnp.where(k.lists[pl.ds(2, 1), tile_at(t)] >= 0, 0.5, 0.0)
            g = k.g[:, tile_at(t)] * alive
            gre, gim = g[:half], g[half:]
            sre, sim = k.s_all[t, 0].astype(F32), k.s_all[t, 1].astype(F32)
            rre, rim = k.r_all[t, 0].astype(F32), k.r_all[t, 1].astype(F32)
            k.rot[:, tile_at(t)] = jnp.concatenate([gre * rre + gim * rim, gim * rre - gre * rim], 0).astype(BF16)
            k.gr_all[:, tile_at(t)] = jnp.concatenate([gre * sre + gim * sim, gim * sre - gre * sim], 0).astype(BF16)

        every(TILES, step)

    def spread(grads, row, base):
        for t in range(TILES):
            k.mm[:, pl.ds(t * TILE, TILE)] = onehot(PAIR, base, k.lists[pl.ds(row, 1), pl.ds(t * TILE, TILE)])
        return lax.dot_general(grads[...], k.mm[...], NT, preferred_element_type=F32).astype(BF16)

    def spread_relations():
        k.gr[pl.ds(width, REL_ROWS - width), :] = jnp.zeros((REL_ROWS - width, REL_WIDE), BF16)

        def step(c):
            k.gr[pl.ds(0, width), tile_at(c, PAIR)] = spread(k.gr_all, 1, c * PAIR)

            @pl.when(c < 2)
            def _():
                near_r(c).start()

            @pl.when(c == 2)
            def _():
                near_r(2).start()
                near_r(3).start()

        every(REL_WIDE // PAIR, step)

    def spread_sources(first, last):
        def step(c):
            k.gs[:, tile_at(c, PAIR)] = spread(k.rot, 0, c * PAIR)
            near_s(2 * c).start()
            near_s(2 * c + 1).start()
            return 0

        lax.fori_loop(first, last, lambda c, _: step(c), 0)

    def relation_part(x):
        near_r(x).wait_recv()
        return (rel_cut(k.gr, here.core, x)[...].astype(F32) + k.r_near[x].astype(F32)).astype(BF16)

    def relation_send(x):
        k.r_part[x] = relation_part(x)
        far_r(x, me_x).start()

    def source_part(u):
        near_s(u).wait_recv()
        return (gs_cut(2 * u + here.core)[...].astype(F32) + k.s_near[u].astype(F32)).astype(BF16)

    def source_send(u):
        k.s_part[u] = source_part(u)
        far_s(u, me_u).start()

    def relation_forward(x):
        wide_r(x, x).wait_recv()
        last_r(here.core, x).start()

    def reduce(src, dst, again):
        edge_grads()
        spread_relations()
        spread_sources(0, 1)
        others(me_x, N_X, relation_send)
        k.r_far[me_x] = relation_part(me_x)
        spread_sources(1, 4)
        others(me_u, N_ROW, source_send)
        k.s_far[me_u] = source_part(me_u)
        others(me_x, N_X, lambda x: far_r(x, x).wait_recv())
        k.r_chunk[...] = total_of(k.r_far, N_X).astype(BF16)
        piece_step(lambda w: sum_r(w, me_q).start())

        others(me_y, N_Y, lambda p: far_a(p, p).wait_recv())
        k.d_part[...] = total_of(k.d_across, N_Y).astype(BF16)
        pair_d.start()

        @pl.when(me_q < PIECES)
        def _():
            k.r_land[me_q] = part(k.r_chunk, me_q)[...]
            others(me_q, N_COL, lambda p: sum_r(me_q, p).wait_recv())
            piece(k.g_all, me_q, here.core, me_x)[...] = total_of(k.r_land, N_COL).astype(BF16)
            others(me_q, N_COL, lambda p: back_r(p, me_q).start())

        others(me_u, N_ROW, lambda u: far_s(u, u).wait_recv())
        share = src[...].astype(F32) - entity_rate * total_of(k.s_far, N_ROW)
        k.src_new[...] = share.astype(BF16)
        src_gather, dst_gather = gathers[1]
        if again:
            src_gather.start()

        others(me_y, N_Y, lambda p: far_o(p, p).wait_recv())
        pair_d.wait_recv()
        share = total_of(k.d_own, N_Y) + k.d_last[...].astype(F32)
        k.dst_new[...] = (dst[...].astype(F32) - entity_rate * share).astype(BF16)
        if again:
            dst_gather.start()

        piece_step(lambda w: back_r(w, w).wait_recv())
        others(me_x, N_X, lambda p: wide_r(p, me_x).start())
        last_r(here.core, me_x).start()
        if again:
            for swap in swaps:
                swap.wait()
            read_lists(1, *lists_away)
            dst_gather.forward()
        others(me_x, N_X, relation_forward)
        if again:
            src_gather.forward()
        every(N_X, lambda x: last_r(1 - here.core, x).wait_recv())
        for start in range(0, rels, CHUNK):
            at = pl.ds(start, min(CHUNK, rels - start))
            grads = k.g_all[pl.ds(0, width), at].astype(F32)
            history = k.his[:, at] + grads * grads
            k.his[:, at] = history
            k.rel[:, at] = k.rel[:, at] - relation_rate * grads / jnp.sqrt(history)

        every(N_X, lambda x: near_r(x).wait_send())
        others(me_x, N_X, lambda x: far_r(x, me_x).wait_send())
        piece_step(lambda w: sum_r(w, me_q).wait_send())

        @pl.when(me_q < PIECES)
        def _():
            others(me_q, N_COL, lambda p: back_r(p, me_q).wait_send())

        others(me_x, N_X, lambda p: wide_r(p, me_x).wait_send())
        every(N_X, lambda x: last_r(here.core, x).wait_send())
        every(N_ROW, lambda u: near_s(u).wait_send())
        others(me_u, N_ROW, lambda u: far_s(u, me_u).wait_send())
        others(me_y, N_Y, lambda p: far_a(p, me_y).wait_send())
        others(me_y, N_Y, lambda p: far_o(p, me_y).wait_send())
        pair_d.wait_send()


    read_lists(0, *lists_here)
    for load in loads:
        load.wait()
    cast_relations()
    pick_relations()
    dst_gather.forward()
    src_gather.forward()
    src_gather.arrive()
    pick_sources()
    score(dst_gather)
    src_gather.drain()
    dst_gather.drain()
    reduce(k.src, k.dst, True)
    src_gather, dst_gather = gathers[1]
    cast_relations()
    pick_relations()
    src_gather.arrive()
    pick_sources()
    score(dst_gather)
    src_gather.drain()
    dst_gather.drain()
    reduce(k.src_new, k.dst_new, False)


def on_device(
    source_table, dest_table, relations, rel_history, src_ids, rel_ids, dst_ids, neg_ids, counts
):
    src, dst = source_table[0].T, dest_table[0].T
    rel, history = relations.T, rel_history.T
    blocks, negs = neg_ids.shape[3:]
    count = jnp.broadcast_to(counts[0, 0][:, None], (2, TILE))
    lists = [src_ids[0, 0], rel_ids[0, 0], dst_ids[0, 0], neg_ids[0, 0].reshape(2 * blocks, negs), count]
    vm, far = pl.BlockSpec(memory_space=pltpu.VMEM), pl.BlockSpec(memory_space=pl.ANY)
    sem = pltpu.SemaphoreType.DMA
    src, dst, rel, history = pl.pallas_call(
        kernel,
        out_shape=[jax.ShapeDtypeStruct(a.shape, a.dtype) for a in (src, dst, rel, history)],
        in_specs=[vm] * 7 + [far] * 2,
        out_specs=[vm] * 4,
        scratch_shapes=[pltpu.VMEM(a.shape, a.dtype) for a in lists]
        + [make(src.shape[0]) for make in SCRATCH.values()]
        + [sem((n,)) for n in SEMS.values() for _ in range(2)]
        + [sem((2,))],
        compiler_params=pltpu.CompilerParams(
            collective_id=0, has_side_effects=True, vmem_limit_bytes=VMEM_BYTES
        ),
    )(src, dst, *lists, rel, history)
    return (src.T[None], dst.T[None], rel.T, history.T)


def solution(mesh):
    placed = (
        P("row", "col", None),
        P("col", "row", None),
        P(),
        P(),
        P("row", "col", None, None),
        P("row", "col", None, None),
        P("row", "col", None, None),
        P("row", "col", None, None, None),
        P("row", "col", None),
    )
    return jax.shard_map(
        on_device,
        mesh=mesh,
        in_specs=placed,
        out_specs=(P("row", "col", None), P("col", "row", None), P(), P()),
        check_vma=False,
    )
```

```python
import functools
import jax
import jax.numpy as jnp
from jax import lax
from jax.experimental import pallas as pl
from jax.experimental.pallas import tpu as pltpu
from jax.sharding import PartitionSpec as P

F32, BF16 = jnp.float32, jnp.bfloat16
MESH = pl.DeviceIdType.MESH
NT = (((1,), (1,)), ((), ()))
entity_rate = 0.3
relation_rate = 0.5
N_Y = 4
N_ROW, N_COL = 8, 16
HALF_COL = 8
TILE, LIVE = 512, 500
TILES = 8
CHUNK, PAIR = 256, 512
SLOTS = TILES * TILE
UNROLL = 4
REL_HALF, REL_CUT, REL_PIECE = 208, 384, 16
REL_ROWS, REL_WIDE = 2 * REL_HALF, N_Y * REL_CUT
PIECES = REL_HALF // REL_PIECE
VMEM_BYTES = 60 * 2**20


class Place:
    def __init__(self):
        self.row, self.col = lax.axis_index("row"), lax.axis_index("col")
        self.core = lax.rem(self.col, 2)
        self.x, self.y = lax.div(self.col, 4), lax.div(self.row, 2)
        self.z_hi = lax.rem(self.row, 2)
        self.xz = lax.div(self.col, 2)
        self.plane = self.x * 4 + self.z_hi * 2 + lax.rem(self.xz, 2)

    def sibling(self, p=None):
        return {"row": self.row, "col": self.col + 1 - 2 * self.core}

    def at_xz(self, p):
        return {"row": self.row, "col": 2 * p + self.core}

    def at_y(self, p):
        return {"row": 2 * p + self.z_hi, "col": self.col}

    def across(self, p=None):
        return {"row": self.row + 1 - 2 * self.z_hi, "col": self.col}

    def at_plane(self, p):
        x, z = lax.div(p, 4), lax.rem(p, 4)
        return {"row": 2 * self.y + lax.div(z, 2), "col": 4 * x + 2 * lax.rem(z, 2) + self.core}

    def partner(self, p=None):
        return {"row": self.row, "col": lax.rem(self.col + HALF_COL, N_COL)}


def others(me, size, act):
    def step(d, _):
        act(lax.rem(me + d, size))
        return 0

    lax.fori_loop(1, size, step, 0)


def every(size, act):
    def step(d, _):
        act(d)
        return 0

    lax.fori_loop(0, size, step, 0)


def send(source, target, sems, peer, slot, device):
    return pltpu.make_async_remote_copy(
        src_ref=source,
        dst_ref=target,
        send_sem=sems[0].at[peer],
        recv_sem=sems[1].at[slot],
        device_id=device,
        device_id_type=MESH,
    )


def meet(here, groups):
    barrier = pltpu.get_barrier_semaphore()
    for me, size, where in groups:
        others(me, size, lambda p: pl.semaphore_signal(barrier, inc=1, device_id=where(p), device_id_type=MESH))
    pl.semaphore_wait(barrier, sum(size - 1 for _, size, _ in groups))


def lanes(ref, width):
    return lambda i: ref.at[:, pl.ds(pl.multiple_of(i * width, width), width)]


class SourceGather:
    def __init__(self, here, mine, table, sems):
        self.here, self.mine, self.to = here, mine, lanes(table, mine.shape[1])
        self.far, self.near = sems[:2], sems[2:]
        self.slot = lambda p: self.to(2 * p + here.core)
        self.back = lambda p: self.to(2 * p + 1 - here.core)

    def far_copy(self, source, target, p, slot):
        return send(source, target, self.far, p, slot, self.here.at_xz(p))

    def near_copy(self, source, target, p):
        return send(source, target, self.near, p, p, self.here.sibling())

    def start(self):
        me = self.here.xz
        others(me, N_ROW, lambda p: self.far_copy(self.mine, self.slot(me), p, me).start())
        self.near_copy(self.mine, self.slot(me), me).start()
        self.slot(me)[...] = self.mine[...]

    def forward(self):
        def step(p):
            self.far_copy(self.mine, self.slot(p), p, p).wait_recv()
            self.near_copy(self.slot(p), self.slot(p), p).start()

        others(self.here.xz, N_ROW, step)

    def arrive(self):
        every(N_ROW, lambda p: self.near_copy(self.mine, self.back(p), p).wait_recv())

    def drain(self):
        me = self.here.xz
        others(me, N_ROW, lambda p: self.far_copy(self.mine, self.slot(me), p, me).wait_send())
        every(N_ROW, lambda p: self.near_copy(self.mine, self.slot(p), p).wait_send())


class DestGather:
    def __init__(self, here, mine, table, sems):
        self.here, self.mine, self.to = here, mine, lanes(table, mine.shape[1])
        self.pair, self.first, self.second = sems[:2], sems[2:4], sems[4:]
        self.slot = lambda p: self.to(2 * p + here.z_hi)
        self.back = lambda p: self.to(2 * p + 1 - here.z_hi)

    def pair_copy(self, target):
        return send(self.mine, target, self.pair, 0, 0, self.here.across())

    def copy(self, sems, source, target, p, slot):
        return send(source, target, sems, p, slot, self.here.at_y(p))

    def start(self):
        me = self.here.y
        self.pair_copy(self.slot(me)).start()
        others(me, N_Y, lambda p: self.copy(self.first, self.mine, self.slot(me), p, me).start())
        self.slot(me)[...] = self.mine[...]

    def forward(self):
        me = self.here.y
        got = self.back(me)
        self.pair_copy(got).wait_recv()
        others(me, N_Y, lambda p: self.copy(self.second, got, got, p, me).start())

    def arrive(self, p):
        self.copy(self.first, self.mine, self.slot(p), p, p).wait_recv()
        self.copy(self.second, self.mine, self.back(p), p, p).wait_recv()

    def drain(self):
        me = self.here.y
        self.pair_copy(self.slot(me)).wait_send()
        others(me, N_Y, lambda p: self.copy(self.first, self.mine, self.slot(me), p, me).wait_send())
        others(me, N_Y, lambda p: self.copy(self.second, self.mine, self.back(me), p, me).wait_send())


def onehot(rows, base, ids):
    at = lax.broadcasted_iota(jnp.int32, (rows, ids.shape[1]), 0) + base
    return jnp.where(at == ids, 1.0, 0.0).astype(BF16)


def total_of(land, size):
    total = land[0].astype(F32)
    for i in range(1, size):
        total = total + land[i].astype(F32)
    return total


def tile_at(t, size=TILE):
    return pl.ds(pl.multiple_of(t * size, size), size)


SCRATCH = dict(
    src_all=lambda w: pltpu.VMEM((w, 2048), BF16),
    dst_all=lambda w: pltpu.VMEM((w, 2048), BF16),
    dnat=lambda w: pltpu.VMEM((PAIR, w), BF16),
    relt=lambda w: pltpu.VMEM((w, REL_WIDE), BF16),
    s_all=lambda w: pltpu.VMEM((TILES, 2, w // 2, TILE), BF16),
    r_all=lambda w: pltpu.VMEM((TILES, 2, w // 2, TILE), BF16),
    rot=lambda w: pltpu.VMEM((w, SLOTS), BF16),
    gr_all=lambda w: pltpu.VMEM((w, SLOTS), BF16),
    g=lambda w: pltpu.VMEM((w, SLOTS), F32),
    mm=lambda w: pltpu.VMEM((PAIR, SLOTS), BF16),
    ohs=lambda w: pltpu.VMEM((2048, TILE), BF16),
    ohr=lambda w: pltpu.VMEM((REL_WIDE, TILE), BF16),
    cnt=lambda w: pltpu.VMEM((TILES // 2, 2048, 128), F32),
    lists=lambda w: pltpu.VMEM((8, SLOTS), jnp.int32),
    gd=lambda w: pltpu.VMEM((w, 2048), BF16),
    gs=lambda w: pltpu.VMEM((w, 2048), BF16),
    gr=lambda w: pltpu.VMEM((REL_ROWS, REL_WIDE), BF16),
    s_near=lambda w: pltpu.VMEM((N_ROW, w, 128), BF16),
    s_part=lambda w: pltpu.VMEM((N_ROW, w, 128), BF16),
    s_far=lambda w: pltpu.VMEM((N_ROW, w, 128), BF16),
    d_across=lambda w: pltpu.VMEM((N_Y, w, 256), BF16),
    d_own=lambda w: pltpu.VMEM((N_Y, w, 256), BF16),
    d_part=lambda w: pltpu.VMEM((w, 256), BF16),
    d_last=lambda w: pltpu.VMEM((w, 256), BF16),
    r_near=lambda w: pltpu.VMEM((N_Y, REL_HALF, REL_CUT), BF16),
    r_part=lambda w: pltpu.VMEM((N_Y, REL_HALF, REL_CUT), BF16),
    r_far=lambda w: pltpu.VMEM((N_Y, REL_HALF, REL_CUT), BF16),
    r_chunk=lambda w: pltpu.VMEM((REL_HALF, REL_CUT), BF16),
    r_land=lambda w: pltpu.VMEM((N_COL, REL_PIECE, REL_CUT), BF16),
)
SEMS = dict(
    swap=5, near_r=N_Y, far_r=N_Y, sum_r=N_COL, back_r=N_COL, wide_r=N_Y, last_r=N_Y, near_s=N_ROW, far_s=N_ROW,
    far_a=N_Y, far_o=N_Y, pair_d=1, src_far=N_ROW, src_near=N_ROW, dst_pair=1, dst_first=N_Y, dst_second=N_Y,
)


class Refs:
    pass


def kernel(*refs):
    refs = list(refs)
    k = Refs()
    for name in ("src", "dst"):
        setattr(k, name, refs.pop(0))
    lists_here = [refs.pop(0) for _ in range(5)]
    rel_in, his_in = refs.pop(0), refs.pop(0)
    for name in ("src_new", "dst_new", "g_0", "g_1"):
        setattr(k, name, refs.pop(0))
    k.rel, k.his = refs.pop(0), refs.pop(0)
    lists_away = [refs.pop(0) for _ in range(5)]
    for name in SCRATCH:
        setattr(k, name, refs.pop(0))
    sems = {name: (refs.pop(0), refs.pop(0)) for name in SEMS}
    load_sems = refs.pop(0)
    width = k.src.shape[0]
    half = width // 2
    rels = rel_in.shape[1]
    here = Place()
    me_y, me_u, me_q = here.y, here.xz, here.plane

    loads = [pltpu.make_async_copy(a, b, load_sems.at[i]) for i, (a, b) in enumerate([(rel_in, k.rel), (his_in, k.his)])]
    for load in loads:
        load.start()
    meet(here, [(here.core, 2, here.sibling), (me_y, N_Y, here.at_y), (me_q, N_COL, here.at_plane)])
    gathers = []
    for src, dst in ((k.src, k.dst), (k.src_new, k.dst_new)):
        gathers.append((
            SourceGather(here, src, k.src_all, sems["src_far"] + sems["src_near"]),
            DestGather(here, dst, k.dst_all, sems["dst_pair"] + sems["dst_first"] + sems["dst_second"]),
        ))
    src_gather, dst_gather = gathers[0]
    dst_gather.start()
    src_gather.start()
    swaps = [send(a, b, sems["swap"], i, i, here.partner()) for i, (a, b) in enumerate(zip(lists_here, lists_away))]
    for swap in swaps:
        swap.start()


    gs_cut, gd_cut = lanes(k.gs, 128), lanes(k.gd, 256)

    def rel_cut(ref, core, x):
        down = pl.ds(pl.multiple_of(core * REL_HALF, REL_PIECE), REL_HALF)
        return ref.at[down, pl.ds(pl.multiple_of(x * REL_CUT, REL_CUT), REL_CUT)]

    def piece(ref, w, core, x):
        down = pl.ds(pl.multiple_of(core * REL_HALF + w * REL_PIECE, REL_PIECE), REL_PIECE)
        return ref.at[down, pl.ds(pl.multiple_of(x * REL_CUT, REL_CUT), REL_CUT)]

    def part(ref, w):
        return ref.at[pl.ds(pl.multiple_of(w * REL_PIECE, REL_PIECE), REL_PIECE), :]

    def same(ref, name, peer, slot, device):
        return send(ref, ref, sems[name], peer, slot, device)

    near_r = lambda y: send(rel_cut(k.gr, 1 - here.core, y), k.r_near.at[y], sems["near_r"], y, y, here.sibling())
    far_r = lambda y, slot: send(k.r_part.at[y], k.r_far.at[slot], sems["far_r"], y, slot, here.at_y(y))
    sum_r = lambda w, slot: send(part(k.r_chunk, w), k.r_land.at[slot], sems["sum_r"], w, slot, here.at_plane(w))
    back_r = lambda g, p, w: same(piece(g, w, here.core, me_y), "back_r", p, w, here.at_plane(p))
    wide_r = lambda g, p, y: same(rel_cut(g, here.core, y), "wide_r", p, y, here.at_y(p))
    last_r = lambda g, core, y: same(rel_cut(g, core, y), "last_r", y, y, here.sibling())
    near_s = lambda u: send(gs_cut(2 * u + 1 - here.core), k.s_near.at[u], sems["near_s"], u, u, here.sibling())
    far_s = lambda u, slot: send(k.s_part.at[u], k.s_far.at[slot], sems["far_s"], u, slot, here.at_xz(u))
    far_a = lambda p, slot: send(
        gd_cut(2 * p + 1 - here.z_hi), k.d_across.at[slot], sems["far_a"], p, slot, here.at_y(p)
    )
    far_o = lambda p, slot: send(gd_cut(2 * p + here.z_hi), k.d_own.at[slot], sems["far_o"], p, slot, here.at_y(p))
    pair_d = send(k.d_part, k.d_last, sems["pair_d"], 0, 0, here.across())

    def piece_step(act):
        def step(w):
            @pl.when(w != me_q)
            def _():
                act(w)

        every(PIECES, step)


    def read_lists(turn, sid, rid, did, nid, count):
        k.lists[...] = jnp.full(k.lists.shape, -1, jnp.int32)
        limit = jnp.broadcast_to(count[:, pl.ds(turn, 1)], (1, LIVE))
        lane = lax.broadcasted_iota(jnp.int32, (1, LIVE), 1)
        for t in range(TILES):
            own, to = pl.ds(t * LIVE, LIVE), pl.ds(t * TILE, LIVE)
            k.lists[pl.ds(0, 1), to] = sid[pl.ds(turn, 1), own]
            k.lists[pl.ds(1, 1), to] = rid[pl.ds(turn, 1), own]
            k.lists[pl.ds(2, 1), to] = jnp.where(lane + t * LIVE < limit, did[pl.ds(turn, 1), own], -1)
        blocks = TILES // 2
        for b in range(blocks):
            ids = nid[turn, pl.ds(b, 1), :]
            low = onehot(128, 0, ids & 127)
            high = onehot(16, 0, ids >> 7)
            total = lax.dot_general(low, high, NT, preferred_element_type=F32) * (1.0 / (2 * LIVE))
            for h in range(16):
                k.cnt[b, pl.ds(h * 128, 128), :] = jnp.broadcast_to(total[:, h : h + 1], (128, 128))

    def cast_relations():
        k.relt[...] = jnp.zeros_like(k.relt)
        k.relt[:, pl.ds(0, rels)] = k.rel[...].astype(BF16)

    def pick_relations():
        def step(t):
            k.ohr[...] = onehot(REL_WIDE, 0, k.lists[pl.ds(1, 1), tile_at(t)])
            r = jnp.dot(k.relt[...], k.ohr[...], preferred_element_type=F32).astype(BF16)
            k.r_all[t, 0] = r[:half]
            k.r_all[t, 1] = r[half:]

        every(TILES, step)

    def pick_sources():
        def step(t):
            sid = k.lists[pl.ds(0, 1), tile_at(t)]
            alive = jnp.where(k.lists[pl.ds(2, 1), tile_at(t)] >= 0, 0.5, 0.0)
            for c in range(2048 // CHUNK):
                k.ohs[pl.ds(c * CHUNK, CHUNK), :] = onehot(CHUNK, c * CHUNK, sid)
            s = jnp.dot(k.src_all[...], k.ohs[...], preferred_element_type=F32)
            sre, sim = s[:half], s[half:]
            rre, rim = k.r_all[t, 0].astype(F32), k.r_all[t, 1].astype(F32)
            k.s_all[t, 0] = sre.astype(BF16)
            k.s_all[t, 1] = sim.astype(BF16)
            rot = jnp.concatenate([sre * rre - sim * rim, sre * rim + sim * rre], 0)
            k.rot[:, tile_at(t)] = (rot * alive).astype(BF16)
            k.g[:, tile_at(t)] = jnp.zeros((width, TILE), F32)

        every(TILES, step)

    def score(dst_gather):
        eye = onehot(CHUNK, 0, lax.broadcasted_iota(jnp.int32, (1, CHUNK), 1))

        def pair_step(d):
            y = lax.rem(me_y + d, N_Y)

            @pl.when(d > 0)
            def _():
                dst_gather.arrive(y)

            for h in range(2):
                some = k.dst_all[:, pl.ds(pl.multiple_of(y * PAIR + h * CHUNK, CHUNK), CHUNK)]
                turned = lax.dot_general(eye, some, NT, preferred_element_type=F32)
                k.dnat[pl.ds(h * CHUNK, CHUNK), :] = turned.astype(BF16)

            def leans(t, h):
                down = pl.ds(h * CHUNK, CHUNK)
                base = y * PAIR + h * CHUNK
                lean = jnp.tanh(jnp.dot(k.dnat[down, :], k.rot[:, tile_at(t)], preferred_element_type=F32))
                share = k.cnt[lax.div(t, 2), pl.ds(pl.multiple_of(base, CHUNK), CHUNK), :]
                wide = lambda a: jnp.concatenate([a] * (TILE // 128), 1)
                hit = lax.broadcasted_iota(jnp.int32, (CHUNK, TILE), 0) == k.lists[pl.ds(2, 1), tile_at(t)] - base
                slope = jnp.where(hit, wide(share + 1), wide(share))
                k.mm[down, tile_at(t)] = (slope * lean + jnp.where(hit, wide(share - 1), wide(share))).astype(BF16)

            def step(u):
                for i in range(UNROLL):
                    for h in range(2):
                        leans(u * UNROLL + i, h)
                for i in range(UNROLL):
                    at = tile_at(u * UNROLL + i)
                    k.g[:, at] += jnp.dot(k.dst_all[:, tile_at(y, PAIR)], k.mm[:, at], preferred_element_type=F32)

            every(TILES // UNROLL, step)
            total = lax.dot_general(k.rot[...], k.mm[...], NT, preferred_element_type=F32)
            k.gd[:, tile_at(y, PAIR)] = total.astype(BF16)

            @pl.when(d > 0)
            def _():
                far_a(y, me_y).start()
                far_o(y, me_y).start()

        every(N_Y, pair_step)
        k.d_across[me_y] = gd_cut(2 * me_y + 1 - here.z_hi)[...]
        k.d_own[me_y] = gd_cut(2 * me_y + here.z_hi)[...]

    def edge_grads():
        def step(t):
            alive = jnp.where(k.lists[pl.ds(2, 1), tile_at(t)] >= 0, 0.5, 0.0)
            g = k.g[:, tile_at(t)] * alive
            gre, gim = g[:half], g[half:]
            sre, sim = k.s_all[t, 0].astype(F32), k.s_all[t, 1].astype(F32)
            rre, rim = k.r_all[t, 0].astype(F32), k.r_all[t, 1].astype(F32)
            k.rot[:, tile_at(t)] = jnp.concatenate([gre * rre + gim * rim, gim * rre - gre * rim], 0).astype(BF16)
            k.gr_all[:, tile_at(t)] = jnp.concatenate([gre * sre + gim * sim, gim * sre - gre * sim], 0).astype(BF16)

        every(TILES, step)

    def spread(grads, row, base):
        hot = k.mm
        for t in range(TILES):
            hot[:, pl.ds(t * TILE, TILE)] = onehot(PAIR, base, k.lists[pl.ds(row, 1), pl.ds(t * TILE, TILE)])
        return lax.dot_general(grads[...], hot[...], NT, preferred_element_type=F32).astype(BF16)

    def spread_relations():
        k.gr[pl.ds(width, REL_ROWS - width), :] = jnp.zeros((REL_ROWS - width, REL_WIDE), BF16)

        def step(c):
            k.gr[pl.ds(0, width), tile_at(c, PAIR)] = spread(k.gr_all, 1, c * PAIR)

            @pl.when(c < 2)
            def _():
                near_r(c).start()

            @pl.when(c == 2)
            def _():
                near_r(2).start()
                near_r(3).start()

        every(REL_WIDE // PAIR, step)

    def spread_sources():
        def step(c):
            k.gs[:, tile_at(c, PAIR)] = spread(k.rot, 0, c * PAIR)
            near_s(2 * c).start()
            near_s(2 * c + 1).start()

            @pl.when(c == 0)
            def _():
                others(me_y, N_Y, relation_send)
                k.r_far[me_y] = relation_part(me_y)

            @pl.when(c > 0)
            def _():
                source_send(2 * c - 2)
                source_send(2 * c - 1)

            @pl.when(c == 2)
            def _():
                others(me_y, N_Y, lambda p: far_a(p, p).wait_recv())
                k.d_part[...] = total_of(k.d_across, N_Y).astype(BF16)
                pair_d.start()

        every(2048 // PAIR, step)
        source_send(N_ROW - 2)
        source_send(N_ROW - 1)

    def relation_part(y):
        near_r(y).wait_recv()
        return (rel_cut(k.gr, here.core, y)[...].astype(F32) + k.r_near[y].astype(F32)).astype(BF16)

    def relation_send(y):
        k.r_part[y] = relation_part(y)
        far_r(y, me_y).start()

    def source_send(u):
        near_s(u).wait_recv()
        both = (gs_cut(2 * u + here.core)[...].astype(F32) + k.s_near[u].astype(F32)).astype(BF16)

        @pl.when(u == me_u)
        def _():
            k.s_far[u] = both

        @pl.when(u != me_u)
        def _():
            k.s_part[u] = both
            far_s(u, me_u).start()

    def reduce(src, dst, g_all, again):
        src_gather, dst_gather = gathers[1]
        edge_grads()
        spread_relations()
        spread_sources()
        others(me_y, N_Y, lambda y: far_r(y, y).wait_recv())
        k.r_chunk[...] = total_of(k.r_far, N_Y).astype(BF16)
        piece_step(lambda w: sum_r(w, me_q).start())

        others(me_y, N_Y, lambda p: far_o(p, p).wait_recv())
        own = total_of(k.d_own, N_Y)

        @pl.when(me_q < PIECES)
        def _():
            k.r_land[me_q] = part(k.r_chunk, me_q)[...]
            others(me_q, N_COL, lambda p: sum_r(me_q, p).wait_recv())
            piece(g_all, me_q, here.core, me_y)[...] = total_of(k.r_land, N_COL).astype(BF16)
            others(me_q, N_COL, lambda p: back_r(g_all, p, me_q).start())

        others(me_u, N_ROW, lambda u: far_s(u, u).wait_recv())
        share = src[...].astype(F32) - entity_rate * total_of(k.s_far, N_ROW)
        k.src_new[...] = share.astype(BF16)
        if again:
            src_gather.start()

        pair_d.wait_recv()
        share = own + k.d_last[...].astype(F32)
        k.dst_new[...] = (dst[...].astype(F32) - entity_rate * share).astype(BF16)

        piece_step(lambda w: back_r(g_all, w, w).wait_recv())
        others(me_y, N_Y, lambda p: wide_r(g_all, p, me_y).start())
        last_r(g_all, here.core, me_y).start()
        if again:
            dst_gather.start()
            for swap in swaps:
                swap.wait()
            read_lists(1, *lists_away)

        def relation_forward(y):
            wide_r(g_all, y, y).wait_recv()
            last_r(g_all, here.core, y).start()

        others(me_y, N_Y, relation_forward)
        if again:
            src_gather.forward()
            dst_gather.forward()
        every(N_Y, lambda y: last_r(g_all, 1 - here.core, y).wait_recv())
        if again:
            for start in range(0, rels, CHUNK):
                at = pl.ds(start, min(CHUNK, rels - start))
                grads = g_all[pl.ds(0, width), at].astype(F32)
                k.rel[:, at] -= relation_rate * grads / jnp.sqrt(k.his[:, at] + grads * grads)

        every(N_Y, lambda y: near_r(y).wait_send())
        others(me_y, N_Y, lambda y: far_r(y, me_y).wait_send())
        piece_step(lambda w: sum_r(w, me_q).wait_send())

        @pl.when(me_q < PIECES)
        def _():
            others(me_q, N_COL, lambda p: back_r(g_all, p, me_q).wait_send())

        others(me_y, N_Y, lambda p: wide_r(g_all, p, me_y).wait_send())
        every(N_Y, lambda y: last_r(g_all, here.core, y).wait_send())
        every(N_ROW, lambda u: near_s(u).wait_send())
        others(me_u, N_ROW, lambda u: far_s(u, me_u).wait_send())
        others(me_y, N_Y, lambda p: far_a(p, me_y).wait_send())
        others(me_y, N_Y, lambda p: far_o(p, me_y).wait_send())
        pair_d.wait_send()


    read_lists(0, *lists_here)
    for load in loads:
        load.wait()
    cast_relations()
    pick_relations()
    dst_gather.forward()
    src_gather.forward()
    src_gather.arrive()
    pick_sources()
    score(dst_gather)
    src_gather.drain()
    dst_gather.drain()
    reduce(k.src, k.dst, k.g_0, True)
    src_gather, dst_gather = gathers[1]
    cast_relations()
    pick_relations()
    src_gather.arrive()
    pick_sources()
    score(dst_gather)
    src_gather.drain()
    dst_gather.drain()
    reduce(k.src_new, k.dst_new, k.g_1, False)


def on_device(
    source_table, dest_table, relations, rel_history, src_ids, rel_ids, dst_ids, neg_ids, counts
):
    src, dst = source_table[0].T, dest_table[0].T
    rel, history = relations.T, rel_history.T
    lists = [src_ids[0, 0], rel_ids[0, 0], dst_ids[0, 0], neg_ids[0, 0], counts[0]]
    vm, far = pl.BlockSpec(memory_space=pltpu.VMEM), pl.BlockSpec(memory_space=pl.ANY)
    sem = pltpu.SemaphoreType.DMA
    grads = jax.ShapeDtypeStruct((REL_ROWS, REL_WIDE), BF16)
    src, dst, *rounds = pl.pallas_call(
        kernel,
        out_shape=[jax.ShapeDtypeStruct(a.shape, a.dtype) for a in (src, dst)] + [grads] * 2,
        in_specs=[vm] * 7 + [far] * 2,
        out_specs=[vm] * 4,
        scratch_shapes=[pltpu.VMEM(a.shape, a.dtype) for a in [rel, history] + lists]
        + [make(src.shape[0]) for make in SCRATCH.values()]
        + [sem((n,)) for n in SEMS.values() for _ in range(2)]
        + [sem((2,))],
        compiler_params=pltpu.CompilerParams(
            collective_id=0, has_side_effects=True, vmem_limit_bytes=VMEM_BYTES
        ),
    )(src, dst, *lists, rel, history)
    for grads in rounds:
        grads = grads[: rel.shape[0], : rel.shape[1]].astype(F32)
        history = history + grads * grads
        rel = rel - relation_rate * grads / jnp.sqrt(history)
    return (src.T[None], dst.T[None], rel.T, history.T)


def solution(mesh):
    placed = (
        P("row", "col", None),
        P("col", "row", None),
        P(),
        P(),
        P("row", "col", None, None),
        P("row", "col", None, None),
        P("row", "col", None, None),
        P("row", "col", None, None, None),
        P("row", "col", None),
    )
    return jax.shard_map(
        on_device,
        mesh=mesh,
        in_specs=placed,
        out_specs=(P("row", "col", None), P("col", "row", None), P(), P()),
        check_vma=False,
    )
```

```python
import functools
import jax
import jax.numpy as jnp
from jax import lax
from jax.experimental import pallas as pl
from jax.experimental.pallas import tpu as pltpu
from jax.sharding import PartitionSpec as P

F32, BF16 = jnp.float32, jnp.bfloat16
MESH = pl.DeviceIdType.MESH
NT = (((1,), (1,)), ((), ()))
entity_rate = 0.3
relation_rate = 0.5
N_Y = 4
N_ROW, N_COL = 8, 16
HALF_COL = 8
TILE, LIVE = 512, 500
TILES = 8
CHUNK, PAIR = 256, 512
SLOTS = TILES * TILE
UNROLL = 4
REL_HALF, REL_CUT, REL_PIECE = 208, 384, 16
REL_ROWS, REL_WIDE = 2 * REL_HALF, N_Y * REL_CUT
PIECES = REL_HALF // REL_PIECE
VMEM_BYTES = 60 * 2**20


class Place:
    def __init__(self):
        self.row, self.col = lax.axis_index("row"), lax.axis_index("col")
        self.core = lax.rem(self.col, 2)
        self.x, self.y = lax.div(self.col, 4), lax.div(self.row, 2)
        self.z_hi = lax.rem(self.row, 2)
        self.xz = lax.div(self.col, 2)
        self.plane = self.x * 4 + self.z_hi * 2 + lax.rem(self.xz, 2)

    def sibling(self, p=None):
        return {"row": self.row, "col": self.col + 1 - 2 * self.core}

    def at_xz(self, p):
        return {"row": self.row, "col": 2 * p + self.core}

    def at_y(self, p):
        return {"row": 2 * p + self.z_hi, "col": self.col}

    def across(self, p=None):
        return {"row": self.row + 1 - 2 * self.z_hi, "col": self.col}

    def at_plane(self, p):
        x, z = lax.div(p, 4), lax.rem(p, 4)
        return {"row": 2 * self.y + lax.div(z, 2), "col": 4 * x + 2 * lax.rem(z, 2) + self.core}

    def partner(self, p=None):
        return {"row": self.row, "col": lax.rem(self.col + HALF_COL, N_COL)}


def others(me, size, act):
    def step(d, _):
        act(lax.rem(me + d, size))
        return 0

    lax.fori_loop(1, size, step, 0)


def every(size, act):
    def step(d, _):
        act(d)
        return 0

    lax.fori_loop(0, size, step, 0)


def send(source, target, sems, peer, slot, device):
    return pltpu.make_async_remote_copy(
        src_ref=source,
        dst_ref=target,
        send_sem=sems[0].at[peer],
        recv_sem=sems[1].at[slot],
        device_id=device,
        device_id_type=MESH,
    )


def meet(here, groups):
    barrier = pltpu.get_barrier_semaphore()
    for me, size, where in groups:
        others(me, size, lambda p: pl.semaphore_signal(barrier, inc=1, device_id=where(p), device_id_type=MESH))
    pl.semaphore_wait(barrier, sum(size - 1 for _, size, _ in groups))


def lanes(ref, width):
    return lambda i: ref.at[:, pl.ds(pl.multiple_of(i * width, width), width)]


class SourceGather:
    def __init__(self, here, mine, table, sems):
        self.here, self.mine, self.to = here, mine, lanes(table, mine.shape[1])
        self.far, self.near = sems[:2], sems[2:]
        self.slot = lambda p: self.to(2 * p + here.core)
        self.back = lambda p: self.to(2 * p + 1 - here.core)

    def far_copy(self, source, target, p, slot):
        return send(source, target, self.far, p, slot, self.here.at_xz(p))

    def near_copy(self, source, target, p):
        return send(source, target, self.near, p, p, self.here.sibling())

    def start(self):
        me = self.here.xz
        others(me, N_ROW, lambda p: self.far_copy(self.mine, self.slot(me), p, me).start())
        self.near_copy(self.mine, self.slot(me), me).start()
        self.slot(me)[...] = self.mine[...]

    def forward(self):
        def step(p):
            self.far_copy(self.mine, self.slot(p), p, p).wait_recv()
            self.near_copy(self.slot(p), self.slot(p), p).start()

        others(self.here.xz, N_ROW, step)

    def arrive(self):
        every(N_ROW, lambda p: self.near_copy(self.mine, self.back(p), p).wait_recv())

    def drain(self):
        me = self.here.xz
        others(me, N_ROW, lambda p: self.far_copy(self.mine, self.slot(me), p, me).wait_send())
        every(N_ROW, lambda p: self.near_copy(self.mine, self.slot(p), p).wait_send())


class DestGather:
    def __init__(self, here, mine, table, sems):
        self.here, self.mine, self.to = here, mine, lanes(table, mine.shape[1])
        self.pair, self.first, self.second = sems[:2], sems[2:4], sems[4:]
        self.slot = lambda p: self.to(2 * p + here.z_hi)
        self.back = lambda p: self.to(2 * p + 1 - here.z_hi)

    def pair_copy(self, target):
        return send(self.mine, target, self.pair, 0, 0, self.here.across())

    def copy(self, sems, source, target, p, slot):
        return send(source, target, sems, p, slot, self.here.at_y(p))

    def start(self):
        me = self.here.y
        self.pair_copy(self.slot(me)).start()
        others(me, N_Y, lambda p: self.copy(self.first, self.mine, self.slot(me), p, me).start())
        self.slot(me)[...] = self.mine[...]

    def forward(self):
        me = self.here.y
        got = self.back(me)
        self.pair_copy(got).wait_recv()
        others(me, N_Y, lambda p: self.copy(self.second, got, got, p, me).start())

    def arrive(self, p):
        self.copy(self.first, self.mine, self.slot(p), p, p).wait_recv()
        self.copy(self.second, self.mine, self.back(p), p, p).wait_recv()

    def drain(self):
        me = self.here.y
        self.pair_copy(self.slot(me)).wait_send()
        others(me, N_Y, lambda p: self.copy(self.first, self.mine, self.slot(me), p, me).wait_send())
        others(me, N_Y, lambda p: self.copy(self.second, self.mine, self.back(me), p, me).wait_send())


def onehot(rows, base, ids):
    at = lax.broadcasted_iota(jnp.int32, (rows, ids.shape[1]), 0) + base
    return jnp.where(at == ids, 1.0, 0.0).astype(BF16)


def total_of(land, size):
    total = land[0].astype(F32)
    for i in range(1, size):
        total = total + land[i].astype(F32)
    return total


def tile_at(t, size=TILE):
    return pl.ds(pl.multiple_of(t * size, size), size)


SCRATCH = dict(
    src_all=lambda w: pltpu.VMEM((w, 2048), BF16),
    dst_all=lambda w: pltpu.VMEM((w, 2048), BF16),
    dnat=lambda w: pltpu.VMEM((PAIR, w), BF16),
    relt=lambda w: pltpu.VMEM((w, REL_WIDE), BF16),
    s_all=lambda w: pltpu.VMEM((TILES, 2, w // 2, TILE), BF16),
    r_all=lambda w: pltpu.VMEM((TILES, 2, w // 2, TILE), BF16),
    rot=lambda w: pltpu.VMEM((w, SLOTS), BF16),
    gr_all=lambda w: pltpu.VMEM((w, SLOTS), BF16),
    g=lambda w: pltpu.VMEM((w, SLOTS), F32),
    mm=lambda w: pltpu.VMEM((PAIR, SLOTS), BF16),
    ohs=lambda w: pltpu.VMEM((2048, TILE), BF16),
    ohr=lambda w: pltpu.VMEM((REL_WIDE, TILE), BF16),
    cnt=lambda w: pltpu.VMEM((TILES // 2, 2048, 128), F32),
    lists=lambda w: pltpu.VMEM((8, SLOTS), jnp.int32),
    gd=lambda w: pltpu.VMEM((w, 2048), BF16),
    gs=lambda w: pltpu.VMEM((w, 2048), BF16),
    gr=lambda w: pltpu.VMEM((REL_ROWS, REL_WIDE), BF16),
    s_near=lambda w: pltpu.VMEM((N_ROW, w, 128), BF16),
    s_part=lambda w: pltpu.VMEM((N_ROW, w, 128), BF16),
    s_far=lambda w: pltpu.VMEM((N_ROW, w, 128), BF16),
    d_across=lambda w: pltpu.VMEM((N_Y, w, 256), BF16),
    d_own=lambda w: pltpu.VMEM((N_Y, w, 256), BF16),
    d_part=lambda w: pltpu.VMEM((w, 256), BF16),
    d_last=lambda w: pltpu.VMEM((w, 256), BF16),
    r_near=lambda w: pltpu.VMEM((N_Y, REL_HALF, REL_CUT), BF16),
    r_part=lambda w: pltpu.VMEM((N_Y, REL_HALF, REL_CUT), BF16),
    r_far=lambda w: pltpu.VMEM((N_Y, REL_HALF, REL_CUT), BF16),
    r_chunk=lambda w: pltpu.VMEM((REL_HALF, REL_CUT), BF16),
    r_land=lambda w: pltpu.VMEM((N_COL, REL_PIECE, REL_CUT), BF16),
)
SEMS = dict(
    swap=5, near_r=N_Y, far_r=N_Y, sum_r=N_COL, back_r=N_COL, wide_r=N_Y, last_r=N_Y, near_s=N_ROW, far_s=N_ROW,
    far_a=N_Y, far_o=N_Y, pair_d=1, src_far=N_ROW, src_near=N_ROW, dst_pair=1, dst_first=N_Y, dst_second=N_Y,
)


class Refs:
    pass


def kernel(*refs):
    refs = list(refs)
    k = Refs()
    for name in ("src", "dst"):
        setattr(k, name, refs.pop(0))
    lists_here = [refs.pop(0) for _ in range(5)]
    rel_in, his_in = refs.pop(0), refs.pop(0)
    for name in ("src_new", "dst_new", "g_0", "g_1"):
        setattr(k, name, refs.pop(0))
    k.rel, k.his = refs.pop(0), refs.pop(0)
    lists_away = [refs.pop(0) for _ in range(5)]
    for name in SCRATCH:
        setattr(k, name, refs.pop(0))
    sems = {name: (refs.pop(0), refs.pop(0)) for name in SEMS}
    load_sems = refs.pop(0)
    width = k.src.shape[0]
    half = width // 2
    rels = rel_in.shape[1]
    here = Place()
    me_y, me_u, me_q = here.y, here.xz, here.plane

    loads = [pltpu.make_async_copy(a, b, load_sems.at[i]) for i, (a, b) in enumerate([(rel_in, k.rel), (his_in, k.his)])]
    for load in loads:
        load.start()
    meet(here, [(here.core, 2, here.sibling), (me_y, N_Y, here.at_y), (me_q, N_COL, here.at_plane)])
    gathers = []
    for src, dst in ((k.src, k.dst), (k.src_new, k.dst_new)):
        gathers.append((
            SourceGather(here, src, k.src_all, sems["src_far"] + sems["src_near"]),
            DestGather(here, dst, k.dst_all, sems["dst_pair"] + sems["dst_first"] + sems["dst_second"]),
        ))
    src_gather, dst_gather = gathers[0]
    dst_gather.start()
    src_gather.start()
    swaps = [send(a, b, sems["swap"], i, i, here.partner()) for i, (a, b) in enumerate(zip(lists_here, lists_away))]
    for swap in swaps:
        swap.start()


    gs_cut, gd_cut = lanes(k.gs, 128), lanes(k.gd, 256)

    def rel_cut(ref, core, x):
        down = pl.ds(pl.multiple_of(core * REL_HALF, REL_PIECE), REL_HALF)
        return ref.at[down, pl.ds(pl.multiple_of(x * REL_CUT, REL_CUT), REL_CUT)]

    def piece(ref, w, core, x):
        down = pl.ds(pl.multiple_of(core * REL_HALF + w * REL_PIECE, REL_PIECE), REL_PIECE)
        return ref.at[down, pl.ds(pl.multiple_of(x * REL_CUT, REL_CUT), REL_CUT)]

    def part(ref, w):
        return ref.at[pl.ds(pl.multiple_of(w * REL_PIECE, REL_PIECE), REL_PIECE), :]

    def same(ref, name, peer, slot, device):
        return send(ref, ref, sems[name], peer, slot, device)

    near_r = lambda y: send(rel_cut(k.gr, 1 - here.core, y), k.r_near.at[y], sems["near_r"], y, y, here.sibling())
    far_r = lambda y, slot: send(k.r_part.at[y], k.r_far.at[slot], sems["far_r"], y, slot, here.at_y(y))
    sum_r = lambda w, slot: send(part(k.r_chunk, w), k.r_land.at[slot], sems["sum_r"], w, slot, here.at_plane(w))
    back_r = lambda g, p, w: same(piece(g, w, here.core, me_y), "back_r", p, w, here.at_plane(p))
    wide_r = lambda g, p, y: same(rel_cut(g, here.core, y), "wide_r", p, y, here.at_y(p))
    last_r = lambda g, core, y: same(rel_cut(g, core, y), "last_r", y, y, here.sibling())
    near_s = lambda u: send(gs_cut(2 * u + 1 - here.core), k.s_near.at[u], sems["near_s"], u, u, here.sibling())
    far_s = lambda u, slot: send(k.s_part.at[u], k.s_far.at[slot], sems["far_s"], u, slot, here.at_xz(u))
    far_a = lambda p, slot: send(
        gd_cut(2 * p + 1 - here.z_hi), k.d_across.at[slot], sems["far_a"], p, slot, here.at_y(p)
    )
    far_o = lambda p, slot: send(gd_cut(2 * p + here.z_hi), k.d_own.at[slot], sems["far_o"], p, slot, here.at_y(p))
    pair_d = send(k.d_part, k.d_last, sems["pair_d"], 0, 0, here.across())

    def piece_step(act):
        def step(w):
            @pl.when(w != me_q)
            def _():
                act(w)

        every(PIECES, step)


    def read_lists(turn, sid, rid, did, nid, count):
        k.lists[...] = jnp.full(k.lists.shape, -1, jnp.int32)
        limit = jnp.broadcast_to(count[:, pl.ds(turn, 1)], (1, LIVE))
        lane = lax.broadcasted_iota(jnp.int32, (1, LIVE), 1)
        for t in range(TILES):
            own, to = pl.ds(t * LIVE, LIVE), pl.ds(t * TILE, LIVE)
            k.lists[pl.ds(0, 1), to] = sid[pl.ds(turn, 1), own]
            k.lists[pl.ds(1, 1), to] = rid[pl.ds(turn, 1), own]
            k.lists[pl.ds(2, 1), to] = jnp.where(lane + t * LIVE < limit, did[pl.ds(turn, 1), own], -1)
        blocks = TILES // 2
        for b in range(blocks):
            ids = nid[turn, pl.ds(b, 1), :]
            low = onehot(128, 0, ids & 127)
            high = onehot(16, 0, ids >> 7)
            total = lax.dot_general(low, high, NT, preferred_element_type=F32) * (1.0 / (2 * LIVE))
            for h in range(16):
                k.cnt[b, pl.ds(h * 128, 128), :] = jnp.broadcast_to(total[:, h : h + 1], (128, 128))

    def cast_relations():
        k.relt[...] = jnp.zeros_like(k.relt)
        k.relt[:, pl.ds(0, rels)] = k.rel[...].astype(BF16)

    def alive(t):
        return jnp.where(k.lists[pl.ds(2, 1), tile_at(t)] >= 0, 0.5, 0.0)

    def both(ref, t):
        return ref[t, 0].astype(F32), ref[t, 1].astype(F32)

    def turn(t, sre, sim, rre, rim):
        rot = jnp.concatenate([sre * rre - sim * rim, sre * rim + sim * rre], 0)
        k.rot[:, tile_at(t)] = (rot * alive(t)).astype(BF16)
        k.g[:, tile_at(t)] = jnp.zeros((width, TILE), F32)

    def pick_relations(last):
        def step(t):
            k.ohr[...] = onehot(REL_WIDE, 0, k.lists[pl.ds(1, 1), tile_at(t)])
            r = jnp.dot(k.relt[...], k.ohr[...], preferred_element_type=F32)
            k.r_all[t, 0] = r[:half].astype(BF16)
            k.r_all[t, 1] = r[half:].astype(BF16)
            if last:
                turn(t, *both(k.s_all, t), r[:half], r[half:])

        every(TILES, step)

    def pick_sources(first, end, last):
        def step(t, _):
            sid = k.lists[pl.ds(0, 1), tile_at(t)]
            for c in range(2048 // CHUNK):
                k.ohs[pl.ds(c * CHUNK, CHUNK), :] = onehot(CHUNK, c * CHUNK, sid)
            s = jnp.dot(k.src_all[...], k.ohs[...], preferred_element_type=F32)
            k.s_all[t, 0] = s[:half].astype(BF16)
            k.s_all[t, 1] = s[half:].astype(BF16)
            if last:
                turn(t, s[:half], s[half:], *both(k.r_all, t))
            return 0

        lax.fori_loop(first, end, step, 0)

    def score(dst_gather):
        eye = onehot(CHUNK, 0, lax.broadcasted_iota(jnp.int32, (1, CHUNK), 1))

        def pair_step(d):
            y = lax.rem(me_y + d, N_Y)

            @pl.when(d > 0)
            def _():
                dst_gather.arrive(y)

            for h in range(2):
                some = k.dst_all[:, pl.ds(pl.multiple_of(y * PAIR + h * CHUNK, CHUNK), CHUNK)]
                turned = lax.dot_general(eye, some, NT, preferred_element_type=F32)
                k.dnat[pl.ds(h * CHUNK, CHUNK), :] = turned.astype(BF16)

            def leans(t, h):
                down = pl.ds(h * CHUNK, CHUNK)
                base = y * PAIR + h * CHUNK
                lean = jnp.tanh(jnp.dot(k.dnat[down, :], k.rot[:, tile_at(t)], preferred_element_type=F32))
                share = k.cnt[lax.div(t, 2), pl.ds(pl.multiple_of(base, CHUNK), CHUNK), :]
                wide = lambda a: jnp.concatenate([a] * (TILE // 128), 1)
                hit = lax.broadcasted_iota(jnp.int32, (CHUNK, TILE), 0) == k.lists[pl.ds(2, 1), tile_at(t)] - base
                slope = jnp.where(hit, wide(share + 1), wide(share))
                k.mm[down, tile_at(t)] = (slope * lean + jnp.where(hit, wide(share - 1), wide(share))).astype(BF16)

            def step(u):
                for i in range(UNROLL):
                    for h in range(2):
                        leans(u * UNROLL + i, h)
                for i in range(UNROLL):
                    at = tile_at(u * UNROLL + i)
                    k.g[:, at] += jnp.dot(k.dst_all[:, tile_at(y, PAIR)], k.mm[:, at], preferred_element_type=F32)

            every(TILES // UNROLL, step)
            total = lax.dot_general(k.rot[...], k.mm[...], NT, preferred_element_type=F32)
            k.gd[:, tile_at(y, PAIR)] = total.astype(BF16)

            @pl.when(d > 0)
            def _():
                far_a(y, me_y).start()
                far_o(y, me_y).start()

        every(N_Y, pair_step)
        k.d_across[me_y] = gd_cut(2 * me_y + 1 - here.z_hi)[...]
        k.d_own[me_y] = gd_cut(2 * me_y + here.z_hi)[...]

    def relation_grads():
        def step(t):
            g = k.g[:, tile_at(t)] * alive(t)
            gre, gim = g[:half], g[half:]
            sre, sim = both(k.s_all, t)
            k.gr_all[:, tile_at(t)] = jnp.concatenate([gre * sre + gim * sim, gim * sre - gre * sim], 0).astype(BF16)

        every(TILES, step)

    def source_grads():
        def step(t):
            g = k.g[:, tile_at(t)] * alive(t)
            gre, gim = g[:half], g[half:]
            rre, rim = both(k.r_all, t)
            k.rot[:, tile_at(t)] = jnp.concatenate([gre * rre + gim * rim, gim * rre - gre * rim], 0).astype(BF16)

        every(TILES, step)

    def spread(grads, row, base):
        hot = k.mm
        for t in range(TILES):
            hot[:, pl.ds(t * TILE, TILE)] = onehot(PAIR, base, k.lists[pl.ds(row, 1), pl.ds(t * TILE, TILE)])
        return lax.dot_general(grads[...], hot[...], NT, preferred_element_type=F32).astype(BF16)

    def spread_relations():
        k.gr[pl.ds(width, REL_ROWS - width), :] = jnp.zeros((REL_ROWS - width, REL_WIDE), BF16)

        def step(c):
            k.gr[pl.ds(0, width), tile_at(c, PAIR)] = spread(k.gr_all, 1, c * PAIR)

            @pl.when(c < 2)
            def _():
                near_r(c).start()

            @pl.when(c == 2)
            def _():
                near_r(2).start()
                near_r(3).start()

        every(REL_WIDE // PAIR, step)

    def spread_sources():
        def step(c):
            k.gs[:, tile_at(c, PAIR)] = spread(k.rot, 0, c * PAIR)
            near_s(2 * c).start()
            near_s(2 * c + 1).start()

            @pl.when(c > 0)
            def _():
                source_send(2 * c - 2)
                source_send(2 * c - 1)

            @pl.when(c == 2)
            def _():
                others(me_y, N_Y, lambda p: far_a(p, p).wait_recv())
                k.d_part[...] = total_of(k.d_across, N_Y).astype(BF16)
                pair_d.start()

        every(2048 // PAIR, step)
        source_send(N_ROW - 2)
        source_send(N_ROW - 1)

    def relation_part(y):
        near_r(y).wait_recv()
        return (rel_cut(k.gr, here.core, y)[...].astype(F32) + k.r_near[y].astype(F32)).astype(BF16)

    def relation_send(y):
        k.r_part[y] = relation_part(y)
        far_r(y, me_y).start()

    def source_send(u):
        near_s(u).wait_recv()
        both = (gs_cut(2 * u + here.core)[...].astype(F32) + k.s_near[u].astype(F32)).astype(BF16)

        @pl.when(u == me_u)
        def _():
            k.s_far[u] = both

        @pl.when(u != me_u)
        def _():
            k.s_part[u] = both
            far_s(u, me_u).start()

    def reduce(src, dst, g_all, again):
        src_gather, dst_gather = gathers[1]
        relation_grads()
        spread_relations()
        source_grads()
        others(me_y, N_Y, relation_send)
        k.r_far[me_y] = relation_part(me_y)
        spread_sources()
        others(me_y, N_Y, lambda y: far_r(y, y).wait_recv())
        k.r_chunk[...] = total_of(k.r_far, N_Y).astype(BF16)
        piece_step(lambda w: sum_r(w, me_q).start())

        others(me_y, N_Y, lambda p: far_o(p, p).wait_recv())
        own = total_of(k.d_own, N_Y)

        @pl.when(me_q < PIECES)
        def _():
            k.r_land[me_q] = part(k.r_chunk, me_q)[...]
            others(me_q, N_COL, lambda p: sum_r(me_q, p).wait_recv())
            piece(g_all, me_q, here.core, me_y)[...] = total_of(k.r_land, N_COL).astype(BF16)
            others(me_q, N_COL, lambda p: back_r(g_all, p, me_q).start())

        others(me_u, N_ROW, lambda u: far_s(u, u).wait_recv())
        share = src[...].astype(F32) - entity_rate * total_of(k.s_far, N_ROW)
        k.src_new[...] = share.astype(BF16)
        if again:
            src_gather.start()

        pair_d.wait_recv()
        share = own + k.d_last[...].astype(F32)
        k.dst_new[...] = (dst[...].astype(F32) - entity_rate * share).astype(BF16)

        piece_step(lambda w: back_r(g_all, w, w).wait_recv())
        others(me_y, N_Y, lambda p: wide_r(g_all, p, me_y).start())
        last_r(g_all, here.core, me_y).start()
        if again:
            dst_gather.start()
            for swap in swaps:
                swap.wait()
            read_lists(1, *lists_away)

        def relation_forward(y):
            wide_r(g_all, y, y).wait_recv()
            last_r(g_all, here.core, y).start()

        if again:
            src_gather.forward()
            dst_gather.forward()
            src_gather.arrive()
            pick_sources(0, TILES // 2, False)
        others(me_y, N_Y, relation_forward)
        if again:
            pick_sources(TILES // 2, TILES, False)
        every(N_Y, lambda y: last_r(g_all, 1 - here.core, y).wait_recv())
        if again:
            for start in range(0, rels, CHUNK):
                at = pl.ds(start, min(CHUNK, rels - start))
                grads = g_all[pl.ds(0, width), at].astype(F32)
                k.rel[:, at] -= relation_rate * grads / jnp.sqrt(k.his[:, at] + grads * grads)

        every(N_Y, lambda y: near_r(y).wait_send())
        others(me_y, N_Y, lambda y: far_r(y, me_y).wait_send())
        piece_step(lambda w: sum_r(w, me_q).wait_send())

        @pl.when(me_q < PIECES)
        def _():
            others(me_q, N_COL, lambda p: back_r(g_all, p, me_q).wait_send())

        others(me_y, N_Y, lambda p: wide_r(g_all, p, me_y).wait_send())
        every(N_Y, lambda y: last_r(g_all, here.core, y).wait_send())
        every(N_ROW, lambda u: near_s(u).wait_send())
        others(me_u, N_ROW, lambda u: far_s(u, me_u).wait_send())
        others(me_y, N_Y, lambda p: far_a(p, me_y).wait_send())
        others(me_y, N_Y, lambda p: far_o(p, me_y).wait_send())
        pair_d.wait_send()


    read_lists(0, *lists_here)
    for load in loads:
        load.wait()
    cast_relations()
    pick_relations(False)
    dst_gather.forward()
    src_gather.forward()
    src_gather.arrive()
    pick_sources(0, TILES, True)
    score(dst_gather)
    src_gather.drain()
    dst_gather.drain()
    reduce(k.src, k.dst, k.g_0, True)
    src_gather, dst_gather = gathers[1]
    cast_relations()
    pick_relations(True)
    score(dst_gather)
    src_gather.drain()
    dst_gather.drain()
    reduce(k.src_new, k.dst_new, k.g_1, False)


def on_device(
    source_table, dest_table, relations, rel_history, src_ids, rel_ids, dst_ids, neg_ids, counts
):
    src, dst = source_table[0].T, dest_table[0].T
    rel, history = relations.T, rel_history.T
    lists = [src_ids[0, 0], rel_ids[0, 0], dst_ids[0, 0], neg_ids[0, 0], counts[0]]
    vm, far = pl.BlockSpec(memory_space=pltpu.VMEM), pl.BlockSpec(memory_space=pl.ANY)
    sem = pltpu.SemaphoreType.DMA
    grads = jax.ShapeDtypeStruct((REL_ROWS, REL_WIDE), BF16)
    src, dst, *rounds = pl.pallas_call(
        kernel,
        out_shape=[jax.ShapeDtypeStruct(a.shape, a.dtype) for a in (src, dst)] + [grads] * 2,
        in_specs=[vm] * 7 + [far] * 2,
        out_specs=[vm] * 4,
        scratch_shapes=[pltpu.VMEM(a.shape, a.dtype) for a in [rel, history] + lists]
        + [make(src.shape[0]) for make in SCRATCH.values()]
        + [sem((n,)) for n in SEMS.values() for _ in range(2)]
        + [sem((2,))],
        compiler_params=pltpu.CompilerParams(
            collective_id=0, has_side_effects=True, vmem_limit_bytes=VMEM_BYTES
        ),
    )(src, dst, *lists, rel, history)
    for grads in rounds:
        grads = grads[: rel.shape[0], : rel.shape[1]].astype(F32)
        history = history + grads * grads
        rel = rel - relation_rate * grads / jnp.sqrt(history)
    return (src.T[None], dst.T[None], rel.T, history.T)


def solution(mesh):
    placed = (
        P("row", "col", None),
        P("col", "row", None),
        P(),
        P(),
        P("row", "col", None, None),
        P("row", "col", None, None),
        P("row", "col", None, None),
        P("row", "col", None, None, None),
        P("row", "col", None),
    )
    return jax.shard_map(
        on_device,
        mesh=mesh,
        in_specs=placed,
        out_specs=(P("row", "col", None), P("col", "row", None), P(), P()),
        check_vma=False,
    )
```

```python
import functools
import jax
import jax.numpy as jnp
from jax import lax
from jax.experimental import pallas as pl
from jax.experimental.pallas import tpu as pltpu
from jax.sharding import PartitionSpec as P

F32, BF16 = jnp.float32, jnp.bfloat16
MESH = pl.DeviceIdType.MESH
NT = (((1,), (1,)), ((), ()))
entity_rate = 0.3
relation_rate = 0.5
N_X, N_Y = 4, 4
N_ROW, N_COL = 8, 16
HALF_COL = 8
TILE, LIVE = 512, 500
TILES = 8
CHUNK, PAIR = 256, 512
SLOTS = TILES * TILE
UNROLL = 8
REL_HALF, REL_CUT, REL_PIECE = 208, 384, 16
REL_ROWS, REL_WIDE = 2 * REL_HALF, N_Y * REL_CUT
PIECES = REL_HALF // REL_PIECE
VMEM_BYTES = 60 * 2**20


class Place:
    def __init__(self):
        self.row, self.col = lax.axis_index("row"), lax.axis_index("col")
        self.core = lax.rem(self.col, 2)
        self.x, self.y = lax.div(self.col, 4), lax.div(self.row, 2)
        self.z_hi = lax.rem(self.row, 2)
        self.xz = lax.div(self.col, 2)
        self.plane = self.x * 4 + self.z_hi * 2 + lax.rem(self.xz, 2)

    def sibling(self, p=None):
        return {"row": self.row, "col": self.col + 1 - 2 * self.core}

    def at_xz(self, p):
        return {"row": self.row, "col": 2 * p + self.core}

    def at_y(self, p):
        return {"row": 2 * p + self.z_hi, "col": self.col}

    def across(self, p=None):
        return {"row": self.row + 1 - 2 * self.z_hi, "col": self.col}

    def at_plane(self, p):
        x, z = lax.div(p, 4), lax.rem(p, 4)
        return {"row": 2 * self.y + lax.div(z, 2), "col": 4 * x + 2 * lax.rem(z, 2) + self.core}

    def partner(self, p=None):
        return {"row": self.row, "col": lax.rem(self.col + HALF_COL, N_COL)}


def others(me, size, act):
    def step(d, _):
        act(lax.rem(me + d, size))
        return 0

    lax.fori_loop(1, size, step, 0)


def every(size, act):
    def step(d, _):
        act(d)
        return 0

    lax.fori_loop(0, size, step, 0)


def send(source, target, sems, peer, slot, device):
    return pltpu.make_async_remote_copy(
        src_ref=source,
        dst_ref=target,
        send_sem=sems[0].at[peer],
        recv_sem=sems[1].at[slot],
        device_id=device,
        device_id_type=MESH,
    )


def meet(here, groups):
    barrier = pltpu.get_barrier_semaphore()
    for me, size, where in groups:
        others(me, size, lambda p: pl.semaphore_signal(barrier, inc=1, device_id=where(p), device_id_type=MESH))
    pl.semaphore_wait(barrier, sum(size - 1 for _, size, _ in groups))


def lanes(ref, width):
    return lambda i: ref.at[:, pl.ds(pl.multiple_of(i * width, width), width)]


class SourceGather:
    def __init__(self, here, mine, table, sems):
        self.here, self.mine, self.to = here, mine, lanes(table, mine.shape[1])
        self.far, self.near = sems[:2], sems[2:]
        self.me, self.x, self.z = here.xz, lax.div(here.xz, 2), lax.rem(here.xz, 2)
        self.mate = self.me + 1 - 2 * self.z
        self.slot = lambda p: self.to(2 * p + here.core)
        self.back = lambda p: self.to(2 * p + 1 - here.core)

    def far_copy(self, source, target, index, peer, slot):
        return send(source, target, self.far, index, slot, self.here.at_xz(peer))

    def near_copy(self, source, target, p):
        return send(source, target, self.near, p, p, self.here.sibling())

    def along_x(self, z, act):
        others(self.x, N_X, lambda x: act(2 * x + z))

    def start(self):
        me, mate = self.me, self.mate
        self.far_copy(self.mine, self.slot(me), mate, mate, me).start()
        self.along_x(self.z, lambda p: self.far_copy(self.mine, self.slot(me), p, p, me).start())
        self.near_copy(self.mine, self.slot(me), me).start()
        self.slot(me)[...] = self.mine[...]

    def got(self, p):
        self.far_copy(self.mine, self.slot(p), p, p, p).wait_recv()
        self.near_copy(self.slot(p), self.slot(p), p).start()

    def forward_mate(self):
        mate = self.mate
        self.far_copy(self.mine, self.slot(mate), mate, mate, mate).wait_recv()

        def step(x):
            self.far_copy(self.slot(mate), self.slot(mate), 2 * x + 1 - self.z, 2 * x + self.z, mate).start()

        others(self.x, N_X, step)
        self.near_copy(self.slot(mate), self.slot(mate), mate).start()

    def forward(self):
        self.along_x(self.z, self.got)
        self.along_x(1 - self.z, self.got)

    def arrive(self):
        every(N_ROW, lambda p: self.near_copy(self.mine, self.back(p), p).wait_recv())

    def drain(self):
        me = self.me
        others(me, N_ROW, lambda p: self.far_copy(self.mine, self.slot(me), p, p, me).wait_send())
        every(N_ROW, lambda p: self.near_copy(self.mine, self.slot(p), p).wait_send())


class DestGather:
    def __init__(self, here, mine, table, sems):
        self.here, self.mine, self.to = here, mine, lanes(table, mine.shape[1])
        self.pair, self.first, self.second = sems[:2], sems[2:4], sems[4:]
        self.slot = lambda p: self.to(2 * p + here.z_hi)
        self.back = lambda p: self.to(2 * p + 1 - here.z_hi)

    def pair_copy(self, target):
        return send(self.mine, target, self.pair, 0, 0, self.here.across())

    def copy(self, sems, source, target, p, slot):
        return send(source, target, sems, p, slot, self.here.at_y(p))

    def start(self):
        me = self.here.y
        self.pair_copy(self.slot(me)).start()
        others(me, N_Y, lambda p: self.copy(self.first, self.mine, self.slot(me), p, me).start())
        self.slot(me)[...] = self.mine[...]

    def forward(self):
        me = self.here.y
        got = self.back(me)
        self.pair_copy(got).wait_recv()
        others(me, N_Y, lambda p: self.copy(self.second, got, got, p, me).start())

    def arrive(self, p):
        self.copy(self.first, self.mine, self.slot(p), p, p).wait_recv()
        self.copy(self.second, self.mine, self.back(p), p, p).wait_recv()

    def drain(self):
        me = self.here.y
        self.pair_copy(self.slot(me)).wait_send()
        others(me, N_Y, lambda p: self.copy(self.first, self.mine, self.slot(me), p, me).wait_send())
        others(me, N_Y, lambda p: self.copy(self.second, self.mine, self.back(me), p, me).wait_send())


def onehot(rows, base, ids):
    at = lax.broadcasted_iota(jnp.int32, (rows, ids.shape[1]), 0) + base
    return jnp.where(at == ids, 1.0, 0.0).astype(BF16)


def total_of(land, size):
    total = land[0].astype(F32)
    for i in range(1, size):
        total = total + land[i].astype(F32)
    return total


def tile_at(t, size=TILE):
    return pl.ds(pl.multiple_of(t * size, size), size)


SCRATCH = dict(
    src_all=lambda w: pltpu.VMEM((w, 2048), BF16),
    dst_all=lambda w: pltpu.VMEM((w, 2048), BF16),
    dnat=lambda w: pltpu.VMEM((PAIR, w), BF16),
    relt=lambda w: pltpu.VMEM((w, REL_WIDE), BF16),
    s_all=lambda w: pltpu.VMEM((TILES, 2, w // 2, TILE), BF16),
    r_all=lambda w: pltpu.VMEM((TILES, 2, w // 2, TILE), BF16),
    rot=lambda w: pltpu.VMEM((w, SLOTS), BF16),
    gr_all=lambda w: pltpu.VMEM((w, SLOTS), BF16),
    g=lambda w: pltpu.VMEM((w, SLOTS), F32),
    mm=lambda w: pltpu.VMEM((PAIR, SLOTS), BF16),
    ohs=lambda w: pltpu.VMEM((2048, TILE), BF16),
    ohr=lambda w: pltpu.VMEM((REL_WIDE, TILE), BF16),
    cnt=lambda w: pltpu.VMEM((TILES // 2, 2048, 128), F32),
    lists=lambda w: pltpu.VMEM((8, SLOTS), jnp.int32),
    gd=lambda w: pltpu.VMEM((w, 2048), BF16),
    gs=lambda w: pltpu.VMEM((w, 2048), BF16),
    gr=lambda w: pltpu.VMEM((REL_ROWS, REL_WIDE), BF16),
    s_near=lambda w: pltpu.VMEM((N_ROW, w, 128), BF16),
    s_part=lambda w: pltpu.VMEM((N_ROW, w, 128), BF16),
    s_far=lambda w: pltpu.VMEM((N_ROW, w, 128), BF16),
    d_across=lambda w: pltpu.VMEM((N_Y, w, 256), BF16),
    d_own=lambda w: pltpu.VMEM((N_Y, w, 256), BF16),
    d_part=lambda w: pltpu.VMEM((w, 256), BF16),
    d_last=lambda w: pltpu.VMEM((w, 256), BF16),
    r_near=lambda w: pltpu.VMEM((N_Y, REL_HALF, REL_CUT), BF16),
    r_part=lambda w: pltpu.VMEM((N_Y, REL_HALF, REL_CUT), BF16),
    r_far=lambda w: pltpu.VMEM((N_Y, REL_HALF, REL_CUT), BF16),
    r_chunk=lambda w: pltpu.VMEM((REL_HALF, REL_CUT), BF16),
    r_land=lambda w: pltpu.VMEM((N_COL, REL_PIECE, REL_CUT), BF16),
)
SEMS = dict(
    swap=5, near_r=N_Y, far_r=N_Y, sum_r=N_COL, back_r=N_COL, wide_r=N_Y, last_r=N_Y, near_s=N_ROW, far_s=N_ROW,
    far_a=N_Y, far_o=N_Y, pair_d=1, src_far=N_ROW, src_near=N_ROW, dst_pair=1, dst_first=N_Y, dst_second=N_Y,
)


class Refs:
    pass


def kernel(*refs):
    refs = list(refs)
    k = Refs()
    for name in ("src", "dst"):
        setattr(k, name, refs.pop(0))
    lists_here = [refs.pop(0) for _ in range(5)]
    rel_in, his_in = refs.pop(0), refs.pop(0)
    for name in ("src_new", "dst_new", "g_0", "g_1"):
        setattr(k, name, refs.pop(0))
    k.rel, k.his = refs.pop(0), refs.pop(0)
    lists_away = [refs.pop(0) for _ in range(5)]
    for name in SCRATCH:
        setattr(k, name, refs.pop(0))
    sems = {name: (refs.pop(0), refs.pop(0)) for name in SEMS}
    load_sems = refs.pop(0)
    width = k.src.shape[0]
    half = width // 2
    rels = rel_in.shape[1]
    here = Place()
    me_y, me_u, me_q = here.y, here.xz, here.plane

    loads = [pltpu.make_async_copy(a, b, load_sems.at[i]) for i, (a, b) in enumerate([(rel_in, k.rel), (his_in, k.his)])]
    for load in loads:
        load.start()
    meet(here, [(here.core, 2, here.sibling), (me_y, N_Y, here.at_y), (me_q, N_COL, here.at_plane)])
    gathers = []
    for src, dst in ((k.src, k.dst), (k.src_new, k.dst_new)):
        gathers.append((
            SourceGather(here, src, k.src_all, sems["src_far"] + sems["src_near"]),
            DestGather(here, dst, k.dst_all, sems["dst_pair"] + sems["dst_first"] + sems["dst_second"]),
        ))
    src_gather, dst_gather = gathers[0]
    src_gather.start()
    dst_gather.start()
    swaps = [send(a, b, sems["swap"], i, i, here.partner()) for i, (a, b) in enumerate(zip(lists_here, lists_away))]
    for swap in swaps:
        swap.start()


    gs_cut, gd_cut = lanes(k.gs, 128), lanes(k.gd, 256)

    def rel_cut(ref, core, x):
        down = pl.ds(pl.multiple_of(core * REL_HALF, REL_PIECE), REL_HALF)
        return ref.at[down, pl.ds(pl.multiple_of(x * REL_CUT, REL_CUT), REL_CUT)]

    def piece(ref, w, core, x):
        down = pl.ds(pl.multiple_of(core * REL_HALF + w * REL_PIECE, REL_PIECE), REL_PIECE)
        return ref.at[down, pl.ds(pl.multiple_of(x * REL_CUT, REL_CUT), REL_CUT)]

    def part(ref, w):
        return ref.at[pl.ds(pl.multiple_of(w * REL_PIECE, REL_PIECE), REL_PIECE), :]

    def same(ref, name, peer, slot, device):
        return send(ref, ref, sems[name], peer, slot, device)

    near_r = lambda y: send(rel_cut(k.gr, 1 - here.core, y), k.r_near.at[y], sems["near_r"], y, y, here.sibling())
    far_r = lambda y, slot: send(k.r_part.at[y], k.r_far.at[slot], sems["far_r"], y, slot, here.at_y(y))
    sum_r = lambda w, slot: send(part(k.r_chunk, w), k.r_land.at[slot], sems["sum_r"], w, slot, here.at_plane(w))
    back_r = lambda g, p, w: same(piece(g, w, here.core, me_y), "back_r", p, w, here.at_plane(p))
    wide_r = lambda g, p, y: same(rel_cut(g, here.core, y), "wide_r", p, y, here.at_y(p))
    last_r = lambda g, core, y: same(rel_cut(g, core, y), "last_r", y, y, here.sibling())
    near_s = lambda u: send(gs_cut(2 * u + 1 - here.core), k.s_near.at[u], sems["near_s"], u, u, here.sibling())
    far_s = lambda u, slot: send(k.s_part.at[u], k.s_far.at[slot], sems["far_s"], u, slot, here.at_xz(u))
    far_a = lambda p, slot: send(
        gd_cut(2 * p + 1 - here.z_hi), k.d_across.at[slot], sems["far_a"], p, slot, here.at_y(p)
    )
    far_o = lambda p, slot: send(gd_cut(2 * p + here.z_hi), k.d_own.at[slot], sems["far_o"], p, slot, here.at_y(p))
    pair_d = send(k.d_part, k.d_last, sems["pair_d"], 0, 0, here.across())

    def piece_step(act):
        def step(w):
            @pl.when(w != me_q)
            def _():
                act(w)

        every(PIECES, step)


    def read_lists(turn, sid, rid, did, nid, count):
        k.lists[...] = jnp.full(k.lists.shape, -1, jnp.int32)
        limit = jnp.broadcast_to(count[:, pl.ds(turn, 1)], (1, LIVE))
        lane = lax.broadcasted_iota(jnp.int32, (1, LIVE), 1)
        for t in range(TILES):
            own, to = pl.ds(t * LIVE, LIVE), pl.ds(t * TILE, LIVE)
            k.lists[pl.ds(0, 1), to] = sid[pl.ds(turn, 1), own]
            k.lists[pl.ds(1, 1), to] = rid[pl.ds(turn, 1), own]
            k.lists[pl.ds(2, 1), to] = jnp.where(lane + t * LIVE < limit, did[pl.ds(turn, 1), own], -1)
        blocks = TILES // 2
        for b in range(blocks):
            ids = nid[turn, pl.ds(b, 1), :]
            low = onehot(128, 0, ids & 127)
            high = onehot(16, 0, ids >> 7)
            total = lax.dot_general(low, high, NT, preferred_element_type=F32) * (1.0 / (2 * LIVE))
            for h in range(16):
                k.cnt[b, pl.ds(h * 128, 128), :] = jnp.broadcast_to(total[:, h : h + 1], (128, 128))

    def cast_relations():
        k.relt[...] = jnp.zeros_like(k.relt)
        k.relt[:, pl.ds(0, rels)] = k.rel[...].astype(BF16)

    def alive(t):
        return jnp.where(k.lists[pl.ds(2, 1), tile_at(t)] >= 0, 0.5, 0.0)

    def both(ref, t):
        return ref[t, 0].astype(F32), ref[t, 1].astype(F32)

    def turn(t, sre, sim, rre, rim):
        rot = jnp.concatenate([sre * rre - sim * rim, sre * rim + sim * rre], 0)
        k.rot[:, tile_at(t)] = (rot * alive(t)).astype(BF16)
        k.g[:, tile_at(t)] = jnp.zeros((width, TILE), F32)

    def pick_relations(first, end, last):
        def step(t, _):
            k.ohr[...] = onehot(REL_WIDE, 0, k.lists[pl.ds(1, 1), tile_at(t)])
            r = jnp.dot(k.relt[...], k.ohr[...], preferred_element_type=F32)
            k.r_all[t, 0] = r[:half].astype(BF16)
            k.r_all[t, 1] = r[half:].astype(BF16)
            if last:
                turn(t, *both(k.s_all, t), r[:half], r[half:])
            return 0

        lax.fori_loop(first, end, step, 0)

    def pick_sources(first, end, last):
        def step(t, _):
            sid = k.lists[pl.ds(0, 1), tile_at(t)]
            for c in range(2048 // CHUNK):
                k.ohs[pl.ds(c * CHUNK, CHUNK), :] = onehot(CHUNK, c * CHUNK, sid)
            s = jnp.dot(k.src_all[...], k.ohs[...], preferred_element_type=F32)
            k.s_all[t, 0] = s[:half].astype(BF16)
            k.s_all[t, 1] = s[half:].astype(BF16)
            if last:
                turn(t, s[:half], s[half:], *both(k.r_all, t))
            return 0

        lax.fori_loop(first, end, step, 0)

    def score(dst_gather):
        eye = onehot(CHUNK, 0, lax.broadcasted_iota(jnp.int32, (1, CHUNK), 1))

        def pair_step(d):
            y = lax.rem(me_y + d, N_Y)

            @pl.when(d > 0)
            def _():
                dst_gather.arrive(y)

            for h in range(2):
                some = k.dst_all[:, pl.ds(pl.multiple_of(y * PAIR + h * CHUNK, CHUNK), CHUNK)]
                turned = lax.dot_general(eye, some, NT, preferred_element_type=F32)
                k.dnat[pl.ds(h * CHUNK, CHUNK), :] = turned.astype(BF16)

            def leans(t, h):
                down = pl.ds(h * CHUNK, CHUNK)
                base = y * PAIR + h * CHUNK
                lean = jnp.tanh(jnp.dot(k.dnat[down, :], k.rot[:, tile_at(t)], preferred_element_type=F32))
                share = k.cnt[lax.div(t, 2), pl.ds(pl.multiple_of(base, CHUNK), CHUNK), :]
                wide = lambda a: jnp.concatenate([a] * (TILE // 128), 1)
                hit = lax.broadcasted_iota(jnp.int32, (CHUNK, TILE), 0) == k.lists[pl.ds(2, 1), tile_at(t)] - base
                slope = jnp.where(hit, wide(share + 1), wide(share))
                k.mm[down, tile_at(t)] = (slope * lean + jnp.where(hit, wide(share - 1), wide(share))).astype(BF16)

            def step(u):
                for i in range(UNROLL):
                    for h in range(2):
                        leans(u * UNROLL + i, h)
                for i in range(UNROLL):
                    at = tile_at(u * UNROLL + i)
                    k.g[:, at] += jnp.dot(k.dst_all[:, tile_at(y, PAIR)], k.mm[:, at], preferred_element_type=F32)

            every(TILES // UNROLL, step)
            total = lax.dot_general(k.rot[...], k.mm[...], NT, preferred_element_type=F32)
            k.gd[:, tile_at(y, PAIR)] = total.astype(BF16)

            @pl.when(d > 0)
            def _():
                far_a(y, me_y).start()
                far_o(y, me_y).start()

        every(N_Y, pair_step)
        k.d_across[me_y] = gd_cut(2 * me_y + 1 - here.z_hi)[...]
        k.d_own[me_y] = gd_cut(2 * me_y + here.z_hi)[...]

    def relation_grads():
        def step(t):
            g = k.g[:, tile_at(t)] * alive(t)
            gre, gim = g[:half], g[half:]
            sre, sim = both(k.s_all, t)
            k.gr_all[:, tile_at(t)] = jnp.concatenate([gre * sre + gim * sim, gim * sre - gre * sim], 0).astype(BF16)

        every(TILES, step)

    def source_grads():
        def step(t):
            g = k.g[:, tile_at(t)] * alive(t)
            gre, gim = g[:half], g[half:]
            rre, rim = both(k.r_all, t)
            k.rot[:, tile_at(t)] = jnp.concatenate([gre * rre + gim * rim, gim * rre - gre * rim], 0).astype(BF16)

        every(TILES, step)

    def spread(grads, row, base):
        hot = k.mm
        for t in range(TILES):
            hot[:, pl.ds(t * TILE, TILE)] = onehot(PAIR, base, k.lists[pl.ds(row, 1), pl.ds(t * TILE, TILE)])
        return lax.dot_general(grads[...], hot[...], NT, preferred_element_type=F32).astype(BF16)

    def spread_relations():
        k.gr[pl.ds(width, REL_ROWS - width), :] = jnp.zeros((REL_ROWS - width, REL_WIDE), BF16)

        def step(c):
            k.gr[pl.ds(0, width), tile_at(c, PAIR)] = spread(k.gr_all, 1, c * PAIR)

            @pl.when(c < 2)
            def _():
                near_r(c).start()

            @pl.when(c == 2)
            def _():
                near_r(2).start()
                near_r(3).start()

        every(REL_WIDE // PAIR, step)

    def spread_sources():
        def step(c):
            k.gs[:, tile_at(c, PAIR)] = spread(k.rot, 0, c * PAIR)
            near_s(2 * c).start()
            near_s(2 * c + 1).start()

            @pl.when(c > 0)
            def _():
                source_send(2 * c - 2)
                source_send(2 * c - 1)

            @pl.when(c == 2)
            def _():
                others(me_y, N_Y, lambda p: far_a(p, p).wait_recv())
                k.d_part[...] = total_of(k.d_across, N_Y).astype(BF16)
                pair_d.start()

        every(2048 // PAIR, step)
        source_send(N_ROW - 2)
        source_send(N_ROW - 1)

    def relation_part(y):
        near_r(y).wait_recv()
        return (rel_cut(k.gr, here.core, y)[...].astype(F32) + k.r_near[y].astype(F32)).astype(BF16)

    def relation_send(y):
        k.r_part[y] = relation_part(y)
        far_r(y, me_y).start()

    def source_send(u):
        near_s(u).wait_recv()
        both = (gs_cut(2 * u + here.core)[...].astype(F32) + k.s_near[u].astype(F32)).astype(BF16)

        @pl.when(u == me_u)
        def _():
            k.s_far[u] = both

        @pl.when(u != me_u)
        def _():
            k.s_part[u] = both
            far_s(u, me_u).start()

    def reduce(src, dst, g_all, again):
        src_gather, dst_gather = gathers[1]
        relation_grads()
        spread_relations()
        source_grads()
        others(me_y, N_Y, relation_send)
        k.r_far[me_y] = relation_part(me_y)
        spread_sources()
        others(me_y, N_Y, lambda y: far_r(y, y).wait_recv())
        k.r_chunk[...] = total_of(k.r_far, N_Y).astype(BF16)
        piece_step(lambda w: sum_r(w, me_q).start())

        others(me_y, N_Y, lambda p: far_o(p, p).wait_recv())
        own = total_of(k.d_own, N_Y)

        @pl.when(me_q < PIECES)
        def _():
            k.r_land[me_q] = part(k.r_chunk, me_q)[...]
            others(me_q, N_COL, lambda p: sum_r(me_q, p).wait_recv())
            piece(g_all, me_q, here.core, me_y)[...] = total_of(k.r_land, N_COL).astype(BF16)
            others(me_q, N_COL, lambda p: back_r(g_all, p, me_q).start())

        others(me_u, N_ROW, lambda u: far_s(u, u).wait_recv())
        share = src[...].astype(F32) - entity_rate * total_of(k.s_far, N_ROW)
        k.src_new[...] = share.astype(BF16)
        if again:
            src_gather.start()

        pair_d.wait_recv()
        share = own + k.d_last[...].astype(F32)
        k.dst_new[...] = (dst[...].astype(F32) - entity_rate * share).astype(BF16)

        piece_step(lambda w: back_r(g_all, w, w).wait_recv())
        others(me_y, N_Y, lambda p: wide_r(g_all, p, me_y).start())
        last_r(g_all, here.core, me_y).start()
        if again:
            dst_gather.start()
            for swap in swaps:
                swap.wait()
            src_gather.forward_mate()
            read_lists(1, *lists_away)

        def relation_forward(y):
            wide_r(g_all, y, y).wait_recv()
            last_r(g_all, here.core, y).start()

        if again:
            src_gather.forward()
            dst_gather.forward()
            src_gather.arrive()
            pick_sources(0, TILES // 2, False)
        others(me_y, N_Y, relation_forward)
        if again:
            pick_sources(TILES // 2, TILES, False)
        every(N_Y, lambda y: last_r(g_all, 1 - here.core, y).wait_recv())
        if again:
            for start in range(0, rels, CHUNK):
                at = pl.ds(start, min(CHUNK, rels - start))
                grads = g_all[pl.ds(0, width), at].astype(F32)
                k.rel[:, at] -= relation_rate * grads / jnp.sqrt(k.his[:, at] + grads * grads)

        every(N_Y, lambda y: near_r(y).wait_send())
        others(me_y, N_Y, lambda y: far_r(y, me_y).wait_send())
        piece_step(lambda w: sum_r(w, me_q).wait_send())

        @pl.when(me_q < PIECES)
        def _():
            others(me_q, N_COL, lambda p: back_r(g_all, p, me_q).wait_send())

        others(me_y, N_Y, lambda p: wide_r(g_all, p, me_y).wait_send())
        every(N_Y, lambda y: last_r(g_all, here.core, y).wait_send())
        every(N_ROW, lambda u: near_s(u).wait_send())
        others(me_u, N_ROW, lambda u: far_s(u, me_u).wait_send())
        others(me_y, N_Y, lambda p: far_a(p, me_y).wait_send())
        others(me_y, N_Y, lambda p: far_o(p, me_y).wait_send())
        pair_d.wait_send()


    read_lists(0, *lists_here)
    for load in loads:
        load.wait()
    cast_relations()
    pick_relations(0, TILES // 4, False)
    src_gather.forward_mate()
    dst_gather.forward()
    pick_relations(TILES // 4, TILES, False)
    src_gather.forward()
    src_gather.arrive()
    pick_sources(0, TILES, True)
    score(dst_gather)
    src_gather.drain()
    dst_gather.drain()
    reduce(k.src, k.dst, k.g_0, True)
    src_gather, dst_gather = gathers[1]
    cast_relations()
    pick_relations(0, TILES, True)
    score(dst_gather)
    src_gather.drain()
    dst_gather.drain()
    reduce(k.src_new, k.dst_new, k.g_1, False)


def on_device(
    source_table, dest_table, relations, rel_history, src_ids, rel_ids, dst_ids, neg_ids, counts
):
    src, dst = source_table[0].T, dest_table[0].T
    rel, history = relations.T, rel_history.T
    lists = [src_ids[0, 0], rel_ids[0, 0], dst_ids[0, 0], neg_ids[0, 0], counts[0]]
    vm, far = pl.BlockSpec(memory_space=pltpu.VMEM), pl.BlockSpec(memory_space=pl.ANY)
    sem = pltpu.SemaphoreType.DMA
    grads = jax.ShapeDtypeStruct((REL_ROWS, REL_WIDE), BF16)
    src, dst, *rounds = pl.pallas_call(
        kernel,
        out_shape=[jax.ShapeDtypeStruct(a.shape, a.dtype) for a in (src, dst)] + [grads] * 2,
        in_specs=[vm] * 7 + [far] * 2,
        out_specs=[vm] * 4,
        scratch_shapes=[pltpu.VMEM(a.shape, a.dtype) for a in [rel, history] + lists]
        + [make(src.shape[0]) for make in SCRATCH.values()]
        + [sem((n,)) for n in SEMS.values() for _ in range(2)]
        + [sem((2,))],
        compiler_params=pltpu.CompilerParams(
            collective_id=0, has_side_effects=True, vmem_limit_bytes=VMEM_BYTES
        ),
    )(src, dst, *lists, rel, history)
    for grads in rounds:
        grads = grads[: rel.shape[0], : rel.shape[1]].astype(F32)
        history = history + grads * grads
        rel = rel - relation_rate * grads / jnp.sqrt(history)
    return (src.T[None], dst.T[None], rel.T, history.T)


def solution(mesh):
    placed = (
        P("row", "col", None),
        P("col", "row", None),
        P(),
        P(),
        P("row", "col", None, None),
        P("row", "col", None, None),
        P("row", "col", None, None),
        P("row", "col", None, None, None),
        P("row", "col", None),
    )
    return jax.shard_map(
        on_device,
        mesh=mesh,
        in_specs=placed,
        out_specs=(P("row", "col", None), P("col", "row", None), P(), P()),
        check_vma=False,
    )
```

```python
import functools
import jax
import jax.numpy as jnp
from jax import lax
from jax.experimental import pallas as pl
from jax.experimental.pallas import tpu as pltpu
from jax.sharding import PartitionSpec as P

F32, BF16 = jnp.float32, jnp.bfloat16
MESH = pl.DeviceIdType.MESH
NT = (((1,), (1,)), ((), ()))
entity_rate = 0.3
relation_rate = 0.5
N_X, N_Y = 4, 4
N_ROW, N_COL = 8, 16
HALF_COL = 8
TILE, LIVE = 512, 500
TILES = 8
CHUNK, PAIR = 256, 512
SLOTS = TILES * TILE
UNROLL = 8
REL_HALF, REL_CUT, REL_PIECE = 208, 384, 16
REL_ROWS, REL_WIDE = 2 * REL_HALF, N_Y * REL_CUT
PIECES = REL_HALF // REL_PIECE
VMEM_BYTES = 60 * 2**20


class Place:
    def __init__(self):
        self.row, self.col = lax.axis_index("row"), lax.axis_index("col")
        self.core = lax.rem(self.col, 2)
        self.x, self.y = lax.div(self.col, 4), lax.div(self.row, 2)
        self.z_hi = lax.rem(self.row, 2)
        self.xz = lax.div(self.col, 2)
        self.plane = self.x * 4 + self.z_hi * 2 + lax.rem(self.xz, 2)

    def sibling(self, p=None):
        return {"row": self.row, "col": self.col + 1 - 2 * self.core}

    def at_xz(self, p):
        return {"row": self.row, "col": 2 * p + self.core}

    def at_y(self, p):
        return {"row": 2 * p + self.z_hi, "col": self.col}

    def across(self, p=None):
        return {"row": self.row + 1 - 2 * self.z_hi, "col": self.col}

    def at_plane(self, p):
        x, z = lax.div(p, 4), lax.rem(p, 4)
        return {"row": 2 * self.y + lax.div(z, 2), "col": 4 * x + 2 * lax.rem(z, 2) + self.core}

    def partner(self, p=None):
        return {"row": self.row, "col": lax.rem(self.col + HALF_COL, N_COL)}


def others(me, size, act):
    def step(d, _):
        act(lax.rem(me + d, size))
        return 0

    lax.fori_loop(1, size, step, 0)


def every(size, act):
    def step(d, _):
        act(d)
        return 0

    lax.fori_loop(0, size, step, 0)


def send(source, target, sems, peer, slot, device):
    return pltpu.make_async_remote_copy(
        src_ref=source,
        dst_ref=target,
        send_sem=sems[0].at[peer],
        recv_sem=sems[1].at[slot],
        device_id=device,
        device_id_type=MESH,
    )


def meet(here, groups):
    barrier = pltpu.get_barrier_semaphore()
    for me, size, where in groups:
        others(me, size, lambda p: pl.semaphore_signal(barrier, inc=1, device_id=where(p), device_id_type=MESH))
    pl.semaphore_wait(barrier, sum(size - 1 for _, size, _ in groups))


def lanes(ref, width):
    return lambda i: ref.at[:, pl.ds(pl.multiple_of(i * width, width), width)]


class SourceGather:
    def __init__(self, here, mine, table, sems):
        self.here, self.mine, self.to = here, mine, lanes(table, mine.shape[1])
        self.far, self.near = sems[:2], sems[2:]
        self.me, self.x, self.z = here.xz, lax.div(here.xz, 2), lax.rem(here.xz, 2)
        self.mate = self.me + 1 - 2 * self.z
        self.slot = lambda p: self.to(2 * p + here.core)
        self.back = lambda p: self.to(2 * p + 1 - here.core)

    def far_copy(self, source, target, index, peer, slot):
        return send(source, target, self.far, index, slot, self.here.at_xz(peer))

    def near_copy(self, source, target, p):
        return send(source, target, self.near, p, p, self.here.sibling())

    def along_x(self, z, act):
        others(self.x, N_X, lambda x: act(2 * x + z))

    def start(self):
        me, mate = self.me, self.mate
        self.far_copy(self.mine, self.slot(me), mate, mate, me).start()
        self.along_x(self.z, lambda p: self.far_copy(self.mine, self.slot(me), p, p, me).start())
        self.near_copy(self.mine, self.slot(me), me).start()
        self.slot(me)[...] = self.mine[...]

    def got(self, p):
        self.far_copy(self.mine, self.slot(p), p, p, p).wait_recv()
        self.near_copy(self.slot(p), self.slot(p), p).start()

    def forward_mate(self):
        mate = self.mate
        self.far_copy(self.mine, self.slot(mate), mate, mate, mate).wait_recv()

        def step(x):
            self.far_copy(self.slot(mate), self.slot(mate), 2 * x + 1 - self.z, 2 * x + self.z, mate).start()

        others(self.x, N_X, step)
        self.near_copy(self.slot(mate), self.slot(mate), mate).start()

    def forward(self):
        self.along_x(self.z, self.got)
        self.along_x(1 - self.z, self.got)

    def arrive(self):
        every(N_ROW, lambda p: self.near_copy(self.mine, self.back(p), p).wait_recv())

    def drain(self):
        me = self.me
        others(me, N_ROW, lambda p: self.far_copy(self.mine, self.slot(me), p, p, me).wait_send())
        every(N_ROW, lambda p: self.near_copy(self.mine, self.slot(p), p).wait_send())


class DestGather:
    def __init__(self, here, mine, table, sems):
        self.here, self.mine, self.to = here, mine, lanes(table, mine.shape[1])
        self.pair, self.first, self.second = sems[:2], sems[2:4], sems[4:]
        self.slot = lambda p: self.to(2 * p + here.z_hi)
        self.back = lambda p: self.to(2 * p + 1 - here.z_hi)

    def pair_copy(self, target):
        return send(self.mine, target, self.pair, 0, 0, self.here.across())

    def copy(self, sems, source, target, p, slot):
        return send(source, target, sems, p, slot, self.here.at_y(p))

    def start(self):
        me = self.here.y
        self.pair_copy(self.slot(me)).start()
        others(me, N_Y, lambda p: self.copy(self.first, self.mine, self.slot(me), p, me).start())
        self.slot(me)[...] = self.mine[...]

    def forward(self):
        me = self.here.y
        got = self.back(me)
        self.pair_copy(got).wait_recv()
        others(me, N_Y, lambda p: self.copy(self.second, got, got, p, me).start())

    def arrive(self, p):
        self.copy(self.first, self.mine, self.slot(p), p, p).wait_recv()
        self.copy(self.second, self.mine, self.back(p), p, p).wait_recv()

    def drain(self):
        me = self.here.y
        self.pair_copy(self.slot(me)).wait_send()
        others(me, N_Y, lambda p: self.copy(self.first, self.mine, self.slot(me), p, me).wait_send())
        others(me, N_Y, lambda p: self.copy(self.second, self.mine, self.back(me), p, me).wait_send())


def onehot(rows, base, ids):
    at = lax.broadcasted_iota(jnp.int32, (rows, ids.shape[1]), 0) + base
    return jnp.where(at == ids, 1.0, 0.0).astype(BF16)


def total_of(land, size):
    total = land[0].astype(F32)
    for i in range(1, size):
        total = total + land[i].astype(F32)
    return total


def tile_at(t, size=TILE):
    return pl.ds(pl.multiple_of(t * size, size), size)


SCRATCH = dict(
    src_all=lambda w: pltpu.VMEM((w, 2048), BF16),
    dst_all=lambda w: pltpu.VMEM((w, 2048), BF16),
    dnat=lambda w: pltpu.VMEM((PAIR, w), BF16),
    relt=lambda w: pltpu.VMEM((w, REL_WIDE), BF16),
    s_all=lambda w: pltpu.VMEM((TILES, 2, w // 2, TILE), BF16),
    r_all=lambda w: pltpu.VMEM((TILES, 2, w // 2, TILE), BF16),
    rot=lambda w: pltpu.VMEM((w, SLOTS), BF16),
    gr_all=lambda w: pltpu.VMEM((w, SLOTS), BF16),
    g=lambda w: pltpu.VMEM((w, SLOTS), F32),
    mm=lambda w: pltpu.VMEM((PAIR, SLOTS), BF16),
    hot=lambda w: pltpu.VMEM((2, 2048, TILE), BF16),
    cnt=lambda w: pltpu.VMEM((TILES // 2, 2048, 128), F32),
    lists=lambda w: pltpu.VMEM((8, SLOTS), jnp.int32),
    gd=lambda w: pltpu.VMEM((w, 2048), BF16),
    gs=lambda w: pltpu.VMEM((w, 2048), BF16),
    gr=lambda w: pltpu.VMEM((REL_ROWS, REL_WIDE), BF16),
    s_near=lambda w: pltpu.VMEM((N_ROW, w, 128), BF16),
    s_part=lambda w: pltpu.VMEM((N_ROW, w, 128), BF16),
    s_far=lambda w: pltpu.VMEM((N_ROW, w, 128), BF16),
    d_across=lambda w: pltpu.VMEM((N_Y, w, 256), BF16),
    d_own=lambda w: pltpu.VMEM((N_Y, w, 256), BF16),
    d_part=lambda w: pltpu.VMEM((w, 256), BF16),
    d_last=lambda w: pltpu.VMEM((w, 256), BF16),
    r_near=lambda w: pltpu.VMEM((N_Y, REL_HALF, REL_CUT), BF16),
    r_part=lambda w: pltpu.VMEM((N_Y, REL_HALF, REL_CUT), BF16),
    r_far=lambda w: pltpu.VMEM((N_Y, REL_HALF, REL_CUT), BF16),
    r_chunk=lambda w: pltpu.VMEM((REL_HALF, REL_CUT), BF16),
    r_land=lambda w: pltpu.VMEM((N_COL, REL_PIECE, REL_CUT), BF16),
)
SEMS = dict(
    swap=5, near_r=N_Y, far_r=N_Y, sum_r=N_COL, back_r=N_COL, wide_r=N_Y, last_r=N_Y, near_s=N_ROW, far_s=N_ROW,
    far_a=N_Y, far_o=N_Y, pair_d=1, src_far=N_ROW, src_near=N_ROW, dst_pair=1, dst_first=N_Y, dst_second=N_Y,
)


class Refs:
    pass


def kernel(*refs):
    refs = list(refs)
    k = Refs()
    for name in ("src", "dst"):
        setattr(k, name, refs.pop(0))
    lists_here = [refs.pop(0) for _ in range(5)]
    rel_in, his_in = refs.pop(0), refs.pop(0)
    for name in ("src_new", "dst_new", "g_0", "g_1"):
        setattr(k, name, refs.pop(0))
    k.rel, k.his = refs.pop(0), refs.pop(0)
    lists_away = [refs.pop(0) for _ in range(5)]
    for name in SCRATCH:
        setattr(k, name, refs.pop(0))
    sems = {name: (refs.pop(0), refs.pop(0)) for name in SEMS}
    load_sems = refs.pop(0)
    width = k.src.shape[0]
    half = width // 2
    rels = rel_in.shape[1]
    here = Place()
    me_y, me_u, me_q = here.y, here.xz, here.plane

    loads = [pltpu.make_async_copy(a, b, load_sems.at[i]) for i, (a, b) in enumerate([(rel_in, k.rel), (his_in, k.his)])]
    for load in loads:
        load.start()
    meet(here, [(here.core, 2, here.sibling), (me_y, N_Y, here.at_y), (me_q, N_COL, here.at_plane)])
    gathers = []
    for src, dst in ((k.src, k.dst), (k.src_new, k.dst_new)):
        gathers.append((
            SourceGather(here, src, k.src_all, sems["src_far"] + sems["src_near"]),
            DestGather(here, dst, k.dst_all, sems["dst_pair"] + sems["dst_first"] + sems["dst_second"]),
        ))
    src_gather, dst_gather = gathers[0]
    src_gather.start()
    dst_gather.start()
    swaps = [send(a, b, sems["swap"], i, i, here.partner()) for i, (a, b) in enumerate(zip(lists_here, lists_away))]
    for swap in swaps:
        swap.start()


    gs_cut, gd_cut = lanes(k.gs, 128), lanes(k.gd, 256)

    def rel_cut(ref, core, x):
        down = pl.ds(pl.multiple_of(core * REL_HALF, REL_PIECE), REL_HALF)
        return ref.at[down, pl.ds(pl.multiple_of(x * REL_CUT, REL_CUT), REL_CUT)]

    def piece(ref, w, core, x):
        down = pl.ds(pl.multiple_of(core * REL_HALF + w * REL_PIECE, REL_PIECE), REL_PIECE)
        return ref.at[down, pl.ds(pl.multiple_of(x * REL_CUT, REL_CUT), REL_CUT)]

    def part(ref, w):
        return ref.at[pl.ds(pl.multiple_of(w * REL_PIECE, REL_PIECE), REL_PIECE), :]

    def same(ref, name, peer, slot, device):
        return send(ref, ref, sems[name], peer, slot, device)

    near_r = lambda y: send(rel_cut(k.gr, 1 - here.core, y), k.r_near.at[y], sems["near_r"], y, y, here.sibling())
    far_r = lambda y, slot: send(k.r_part.at[y], k.r_far.at[slot], sems["far_r"], y, slot, here.at_y(y))
    sum_r = lambda w, slot: send(part(k.r_chunk, w), k.r_land.at[slot], sems["sum_r"], w, slot, here.at_plane(w))
    back_r = lambda g, p, w: same(piece(g, w, here.core, me_y), "back_r", p, w, here.at_plane(p))
    wide_r = lambda g, p, y: same(rel_cut(g, here.core, y), "wide_r", p, y, here.at_y(p))
    last_r = lambda g, core, y: same(rel_cut(g, core, y), "last_r", y, y, here.sibling())
    near_s = lambda u: send(gs_cut(2 * u + 1 - here.core), k.s_near.at[u], sems["near_s"], u, u, here.sibling())
    far_s = lambda u, slot: send(k.s_part.at[u], k.s_far.at[slot], sems["far_s"], u, slot, here.at_xz(u))
    far_a = lambda p, slot: send(
        gd_cut(2 * p + 1 - here.z_hi), k.d_across.at[slot], sems["far_a"], p, slot, here.at_y(p)
    )
    far_o = lambda p, slot: send(gd_cut(2 * p + here.z_hi), k.d_own.at[slot], sems["far_o"], p, slot, here.at_y(p))
    pair_d = send(k.d_part, k.d_last, sems["pair_d"], 0, 0, here.across())

    def piece_step(act):
        def step(w):
            @pl.when(w != me_q)
            def _():
                act(w)

        every(PIECES, step)


    def read_lists(turn, sid, rid, did, nid, count):
        k.lists[...] = jnp.full(k.lists.shape, -1, jnp.int32)
        limit = jnp.broadcast_to(count[:, pl.ds(turn, 1)], (1, LIVE))
        lane = lax.broadcasted_iota(jnp.int32, (1, LIVE), 1)
        for t in range(TILES):
            own, to = pl.ds(t * LIVE, LIVE), pl.ds(t * TILE, LIVE)
            k.lists[pl.ds(0, 1), to] = sid[pl.ds(turn, 1), own]
            k.lists[pl.ds(1, 1), to] = rid[pl.ds(turn, 1), own]
            k.lists[pl.ds(2, 1), to] = jnp.where(lane + t * LIVE < limit, did[pl.ds(turn, 1), own], -1)
        blocks = TILES // 2
        for b in range(blocks):
            ids = nid[turn, pl.ds(b, 1), :]
            low = onehot(128, 0, ids & 127)
            high = onehot(16, 0, ids >> 7)
            total = lax.dot_general(low, high, NT, preferred_element_type=F32) * (1.0 / (2 * LIVE))
            for h in range(16):
                k.cnt[b, pl.ds(h * 128, 128), :] = jnp.broadcast_to(total[:, h : h + 1], (128, 128))

    def cast_relations():
        k.relt[...] = jnp.zeros_like(k.relt)
        k.relt[:, pl.ds(0, rels)] = k.rel[...].astype(BF16)

    def alive(t):
        return jnp.where(k.lists[pl.ds(2, 1), tile_at(t)] >= 0, 0.5, 0.0)

    def both(ref, t):
        return ref[t, 0].astype(F32), ref[t, 1].astype(F32)

    def turn(t, sre, sim, rre, rim):
        rot = jnp.concatenate([sre * rre - sim * rim, sre * rim + sim * rre], 0)
        k.rot[:, tile_at(t)] = (rot * alive(t)).astype(BF16)
        k.g[:, tile_at(t)] = jnp.zeros((width, TILE), F32)

    def in_pairs(first, end, act):
        def step(t, _):
            for i in range(2):
                act(2 * t + i, k.hot.at[i])
            return 0

        lax.fori_loop(first // 2, end // 2, step, 0)

    def pick_relations(first, end, last):
        def step(t, hot):
            hot = hot.at[pl.ds(0, REL_WIDE), :]
            hot[...] = onehot(REL_WIDE, 0, k.lists[pl.ds(1, 1), tile_at(t)])
            r = jnp.dot(k.relt[...], hot[...], preferred_element_type=F32)
            k.r_all[t, 0] = r[:half].astype(BF16)
            k.r_all[t, 1] = r[half:].astype(BF16)
            if last:
                turn(t, *both(k.s_all, t), r[:half], r[half:])

        in_pairs(first, end, step)

    def pick_sources(first, end, last):
        def step(t, hot):
            sid = k.lists[pl.ds(0, 1), tile_at(t)]
            for c in range(2048 // CHUNK):
                hot[pl.ds(c * CHUNK, CHUNK), :] = onehot(CHUNK, c * CHUNK, sid)
            s = jnp.dot(k.src_all[...], hot[...], preferred_element_type=F32)
            k.s_all[t, 0] = s[:half].astype(BF16)
            k.s_all[t, 1] = s[half:].astype(BF16)
            if last:
                turn(t, s[:half], s[half:], *both(k.r_all, t))

        in_pairs(first, end, step)

    def score(dst_gather):
        eye = onehot(CHUNK, 0, lax.broadcasted_iota(jnp.int32, (1, CHUNK), 1))

        def pair_step(d):
            y = lax.rem(me_y + d, N_Y)

            @pl.when(d > 0)
            def _():
                dst_gather.arrive(y)

            for h in range(2):
                some = k.dst_all[:, pl.ds(pl.multiple_of(y * PAIR + h * CHUNK, CHUNK), CHUNK)]
                turned = lax.dot_general(eye, some, NT, preferred_element_type=F32)
                k.dnat[pl.ds(h * CHUNK, CHUNK), :] = turned.astype(BF16)

            def leans(t, h):
                down = pl.ds(h * CHUNK, CHUNK)
                base = y * PAIR + h * CHUNK
                lean = jnp.tanh(jnp.dot(k.dnat[down, :], k.rot[:, tile_at(t)], preferred_element_type=F32))
                share = k.cnt[lax.div(t, 2), pl.ds(pl.multiple_of(base, CHUNK), CHUNK), :]
                wide = lambda a: jnp.concatenate([a] * (TILE // 128), 1)
                hit = lax.broadcasted_iota(jnp.int32, (CHUNK, TILE), 0) == k.lists[pl.ds(2, 1), tile_at(t)] - base
                slope = jnp.where(hit, wide(share + 1), wide(share))
                k.mm[down, tile_at(t)] = (slope * lean + jnp.where(hit, wide(share - 1), wide(share))).astype(BF16)

            def step(u):
                for i in range(UNROLL):
                    for h in range(2):
                        leans(u * UNROLL + i, h)
                for i in range(UNROLL):
                    at = tile_at(u * UNROLL + i)
                    k.g[:, at] += jnp.dot(k.dst_all[:, tile_at(y, PAIR)], k.mm[:, at], preferred_element_type=F32)

            every(TILES // UNROLL, step)
            total = lax.dot_general(k.rot[...], k.mm[...], NT, preferred_element_type=F32)
            k.gd[:, tile_at(y, PAIR)] = total.astype(BF16)

            @pl.when(d > 0)
            def _():
                far_a(y, me_y).start()
                far_o(y, me_y).start()

        every(N_Y, pair_step)
        k.d_across[me_y] = gd_cut(2 * me_y + 1 - here.z_hi)[...]
        k.d_own[me_y] = gd_cut(2 * me_y + here.z_hi)[...]

    def relation_grads():
        def step(t):
            g = k.g[:, tile_at(t)] * alive(t)
            gre, gim = g[:half], g[half:]
            sre, sim = both(k.s_all, t)
            k.gr_all[:, tile_at(t)] = jnp.concatenate([gre * sre + gim * sim, gim * sre - gre * sim], 0).astype(BF16)

        every(TILES, step)

    def source_grads():
        def step(t):
            g = k.g[:, tile_at(t)] * alive(t)
            gre, gim = g[:half], g[half:]
            rre, rim = both(k.r_all, t)
            k.rot[:, tile_at(t)] = jnp.concatenate([gre * rre + gim * rim, gim * rre - gre * rim], 0).astype(BF16)

        every(TILES, step)

    def spread(grads, row, base):
        hot = k.mm
        for t in range(TILES):
            hot[:, pl.ds(t * TILE, TILE)] = onehot(PAIR, base, k.lists[pl.ds(row, 1), pl.ds(t * TILE, TILE)])
        return lax.dot_general(grads[...], hot[...], NT, preferred_element_type=F32).astype(BF16)

    def spread_relations():
        k.gr[pl.ds(width, REL_ROWS - width), :] = jnp.zeros((REL_ROWS - width, REL_WIDE), BF16)

        def step(c):
            k.gr[pl.ds(0, width), tile_at(c, PAIR)] = spread(k.gr_all, 1, c * PAIR)

            @pl.when(c < 2)
            def _():
                near_r(c).start()

            @pl.when(c == 2)
            def _():
                near_r(2).start()
                near_r(3).start()

        every(REL_WIDE // PAIR, step)

    def spread_sources():
        def step(c):
            k.gs[:, tile_at(c, PAIR)] = spread(k.rot, 0, c * PAIR)
            near_s(2 * c).start()
            near_s(2 * c + 1).start()

            @pl.when(c > 0)
            def _():
                source_send(2 * c - 2)
                source_send(2 * c - 1)

            @pl.when(c == 2)
            def _():
                others(me_y, N_Y, lambda p: far_a(p, p).wait_recv())
                k.d_part[...] = total_of(k.d_across, N_Y).astype(BF16)
                pair_d.start()

        every(2048 // PAIR, step)
        source_send(N_ROW - 2)
        source_send(N_ROW - 1)

    def relation_part(y):
        near_r(y).wait_recv()
        return (rel_cut(k.gr, here.core, y)[...].astype(F32) + k.r_near[y].astype(F32)).astype(BF16)

    def relation_send(y):
        k.r_part[y] = relation_part(y)
        far_r(y, me_y).start()

    def source_send(u):
        near_s(u).wait_recv()
        both = (gs_cut(2 * u + here.core)[...].astype(F32) + k.s_near[u].astype(F32)).astype(BF16)

        @pl.when(u == me_u)
        def _():
            k.s_far[u] = both

        @pl.when(u != me_u)
        def _():
            k.s_part[u] = both
            far_s(u, me_u).start()

    def reduce(src, dst, g_all, again):
        src_gather, dst_gather = gathers[1]
        relation_grads()
        spread_relations()
        source_grads()
        others(me_y, N_Y, relation_send)
        k.r_far[me_y] = relation_part(me_y)
        spread_sources()
        others(me_y, N_Y, lambda y: far_r(y, y).wait_recv())
        k.r_chunk[...] = total_of(k.r_far, N_Y).astype(BF16)
        piece_step(lambda w: sum_r(w, me_q).start())

        @pl.when(me_q < PIECES)
        def _():
            k.r_land[me_q] = part(k.r_chunk, me_q)[...]
            others(me_q, N_COL, lambda p: sum_r(me_q, p).wait_recv())
            piece(g_all, me_q, here.core, me_y)[...] = total_of(k.r_land, N_COL).astype(BF16)
            others(me_q, N_COL, lambda p: back_r(g_all, p, me_q).start())

        def update_source():
            others(me_u, N_ROW, lambda u: far_s(u, u).wait_recv())
            share = src[...].astype(F32) - entity_rate * total_of(k.s_far, N_ROW)
            k.src_new[...] = share.astype(BF16)

        if again:
            update_source()
            src_gather.start()

        piece_step(lambda w: back_r(g_all, w, w).wait_recv())
        others(me_y, N_Y, lambda p: wide_r(g_all, p, me_y).start())
        last_r(g_all, here.core, me_y).start()
        if not again:
            update_source()

        others(me_y, N_Y, lambda p: far_o(p, p).wait_recv())
        pair_d.wait_recv()
        share = total_of(k.d_own, N_Y) + k.d_last[...].astype(F32)
        k.dst_new[...] = (dst[...].astype(F32) - entity_rate * share).astype(BF16)
        if again:
            dst_gather.start()
            for swap in swaps:
                swap.wait()
            src_gather.forward_mate()
            read_lists(1, *lists_away)

        def relation_forward(y):
            wide_r(g_all, y, y).wait_recv()
            last_r(g_all, here.core, y).start()

        if again:
            src_gather.forward()
            dst_gather.forward()
            src_gather.arrive()
            pick_sources(0, TILES // 2, False)
        others(me_y, N_Y, relation_forward)
        if again:
            pick_sources(TILES // 2, TILES, False)
        every(N_Y, lambda y: last_r(g_all, 1 - here.core, y).wait_recv())
        if again:
            for start in range(0, rels, CHUNK):
                at = pl.ds(start, min(CHUNK, rels - start))
                grads = g_all[pl.ds(0, width), at].astype(F32)
                k.rel[:, at] -= relation_rate * grads / jnp.sqrt(k.his[:, at] + grads * grads)

        every(N_Y, lambda y: near_r(y).wait_send())
        others(me_y, N_Y, lambda y: far_r(y, me_y).wait_send())
        piece_step(lambda w: sum_r(w, me_q).wait_send())

        @pl.when(me_q < PIECES)
        def _():
            others(me_q, N_COL, lambda p: back_r(g_all, p, me_q).wait_send())

        others(me_y, N_Y, lambda p: wide_r(g_all, p, me_y).wait_send())
        every(N_Y, lambda y: last_r(g_all, here.core, y).wait_send())
        every(N_ROW, lambda u: near_s(u).wait_send())
        others(me_u, N_ROW, lambda u: far_s(u, me_u).wait_send())
        others(me_y, N_Y, lambda p: far_a(p, me_y).wait_send())
        others(me_y, N_Y, lambda p: far_o(p, me_y).wait_send())
        pair_d.wait_send()


    read_lists(0, *lists_here)
    for load in loads:
        load.wait()
    cast_relations()
    pick_relations(0, TILES // 4, False)
    src_gather.forward_mate()
    dst_gather.forward()
    pick_relations(TILES // 4, TILES, False)
    src_gather.forward()
    src_gather.arrive()
    pick_sources(0, TILES, True)
    score(dst_gather)
    src_gather.drain()
    dst_gather.drain()
    reduce(k.src, k.dst, k.g_0, True)
    src_gather, dst_gather = gathers[1]
    cast_relations()
    pick_relations(0, TILES, True)
    score(dst_gather)
    src_gather.drain()
    dst_gather.drain()
    reduce(k.src_new, k.dst_new, k.g_1, False)


def on_device(
    source_table, dest_table, relations, rel_history, src_ids, rel_ids, dst_ids, neg_ids, counts
):
    src, dst = source_table[0].T, dest_table[0].T
    rel, history = relations.T, rel_history.T
    lists = [src_ids[0, 0], rel_ids[0, 0], dst_ids[0, 0], neg_ids[0, 0], counts[0]]
    vm, far = pl.BlockSpec(memory_space=pltpu.VMEM), pl.BlockSpec(memory_space=pl.ANY)
    sem = pltpu.SemaphoreType.DMA
    grads = jax.ShapeDtypeStruct((REL_ROWS, REL_WIDE), BF16)
    src, dst, *rounds = pl.pallas_call(
        kernel,
        out_shape=[jax.ShapeDtypeStruct(a.shape, a.dtype) for a in (src, dst)] + [grads] * 2,
        in_specs=[vm] * 7 + [far] * 2,
        out_specs=[vm] * 4,
        scratch_shapes=[pltpu.VMEM(a.shape, a.dtype) for a in [rel, history] + lists]
        + [make(src.shape[0]) for make in SCRATCH.values()]
        + [sem((n,)) for n in SEMS.values() for _ in range(2)]
        + [sem((2,))],
        compiler_params=pltpu.CompilerParams(
            collective_id=0, has_side_effects=True, vmem_limit_bytes=VMEM_BYTES
        ),
    )(src, dst, *lists, rel, history)
    for grads in rounds:
        grads = grads[: rel.shape[0], : rel.shape[1]].astype(F32)
        history = history + grads * grads
        rel = rel - relation_rate * grads / jnp.sqrt(history)
    return (src.T[None], dst.T[None], rel.T, history.T)


def solution(mesh):
    placed = (
        P("row", "col", None),
        P("col", "row", None),
        P(),
        P(),
        P("row", "col", None, None),
        P("row", "col", None, None),
        P("row", "col", None, None),
        P("row", "col", None, None, None),
        P("row", "col", None),
    )
    return jax.shard_map(
        on_device,
        mesh=mesh,
        in_specs=placed,
        out_specs=(P("row", "col", None), P("col", "row", None), P(), P()),
        check_vma=False,
    )
```
